1024 devices in a mesh: ab: 128 (over z, y), cd: 8 (over x, core).
Axes of the slice: x: 4, y: 4, z: 32, core: 2. Of those that a mesh axis runs over, the one named last changes fastest.
Arguments:
- integrals: float32 [131072, 4096], P('ab', 'cd'), may hold values from -0.375 to 0.375
- amplitudes: float32 [1024, 4096], P('ab', 'cd'), may hold values from -6 to 6
- allowed: int32 [1024, 32], P('ab', 'cd'), may hold values 0 or 1
Outputs:
- residual: float32 [1024, 131072], P('cd', 'ab')
The draws below stay inside these ranges and needn't reach their ends.
All inputs are finite; a program needn't handle non-finite values. No bound on the sum of `allowed` on one device may be relied on, other than what follows from the above.
Results may differ from the reference program's by a relative error of at most 0.00007.
Values sent between devices are 32-bit elements; how exact they have to be, the bound alone decides.
No kernel may reach another device: no remote copies, remote signals or barrier semaphores. Data moves between devices by JAX's collectives and lax.ppermute only.
A program may use at most 32 MiB of HBM per device.

```python
import jax
import jax.numpy as jnp
from jax import lax

BLK = 128
A_DEV = 1024
AB = 131072
CD = 4096
PAIRS = 1024
N_AB = 128


def place_ends(entries, rng, low, high):
    dims = entries.shape
    spot = [jax.random.randint(jax.random.fold_in(rng, axis), (), 0, dims[axis]) for axis in range(len(dims))]
    entries = entries.at[tuple(spot)].set(low)
    longest = dims.index(max(dims))
    spot[longest] = (spot[longest] + 1) % dims[longest]
    return entries.at[tuple(spot)].set(high)


def with_spikes(array, own_key, source, target, parts, factor):
    def block_of(axis_at):
        return (jnp.arange(array.shape[axis_at]) // (array.shape[axis_at] // parts)).reshape((-1,) + (1,) * (array.ndim - 1 - axis_at))

    one_side = jax.random.permutation(own_key, parts)[block_of(target)]
    second = (block_of(target) + parts // 2) % parts
    return jnp.where((block_of(source) == one_side) | (block_of(source) == second), factor * array, array)


def shard_levels(key, shape, cuts, low, top_value):
    gain, own = 1.0, jax.random.fold_in(key, 6)
    for dim, shards_of in cuts:
        heights = jnp.exp(jax.random.uniform(jax.random.fold_in(own, dim), (shards_of,), jnp.float32, low / len(cuts), top_value / len(cuts)))
        gain = gain * jnp.repeat(heights, shape[dim] // shards_of).reshape([-1 if axis == dim else 1 for axis in range(len(shape))])
    return gain


def gaussian(key, dims, width, reach, cuts=(), kind=jnp.bfloat16):
    drawn = width * jax.random.normal(key, dims, jnp.float32)
    if cuts:
        drawn = drawn * shard_levels(key, dims, cuts, -0.22, 0.18)
    return jnp.clip(drawn, -reach, reach).astype(kind)


def bell_draw_with(own_key, extent, width, most, shards, heavy, dtype=jnp.bfloat16):
    array = width * jax.random.normal(own_key, extent, jnp.float32)
    if shards:
        array = array * shard_levels(own_key, extent, shards, -0.22, 0.18)
    return jnp.clip(with_spikes(array, jax.random.fold_in(own_key, 3), *heavy), -most, most).astype(dtype)


def setup_inputs(seed: int = 0) -> dict:
    seeds = jax.random.split(jax.random.key(seed), 4)
    integrals = bell_draw_with(seeds[0], (AB, CD), CD ** -0.5, 0.375, ((0, 128), (1, 8)), (1, 0, 128, 5.5), jnp.float32)
    amplitudes = gaussian(seeds[1], (PAIRS, CD), 1.0, 6.0, ((0, 128), (1, 8)), jnp.float32)
    allowed = place_ends((jax.random.randint(seeds[2], (AB // BLK, CD // BLK), 0, 8) < 1).astype(jnp.int32), jax.random.fold_in(seeds[2], 1), 0, 1)
    return dict(integrals=integrals, amplitudes=amplitudes, allowed=allowed)


def reference(integrals, amplitudes, allowed):
    slab = integrals.reshape(N_AB, A_DEV, CD)
    flags = allowed.reshape(N_AB, A_DEV // BLK, CD // BLK)

    def one_block(pack):
        rows, marks = pack
        weights = marks.astype(jnp.float32)[:, None, :, None]
        kept = (rows.reshape(A_DEV // BLK, BLK, CD // BLK, BLK) * weights).reshape(A_DEV, CD)
        return lax.dot_general(amplitudes, kept, (((1,), (1,)), ((), ())), precision=lax.Precision.HIGHEST, preferred_element_type=jnp.float32)

    blocks = lax.map(one_block, (slab, flags))
    return jnp.transpose(blocks, (1, 0, 2)).reshape(PAIRS, AB)
```

```python
import jax
import jax.numpy as jnp
from jax import lax
from jax.experimental import pallas as pl
from jax.experimental.pallas import tpu as pltpu
from jax.sharding import Mesh, PartitionSpec as P

BLK = 128
NT = (((1,), (1,)), ((), ()))
COLS = 256


def split(wide):
    high = wide.astype(jnp.bfloat16)
    return high, (wide - high.astype(jnp.float32)).astype(jnp.bfloat16)


def ladder_body(par_ref, allowed_ref, t_ref, v_ref, *rest):
    got_ref = rest[0] if len(rest) == 4 else None
    out_ref, th_ref, tl_ref = rest[-3:]
    step = pl.program_id(0)

    @pl.when(step == 0)
    def _():
        for xx in range(4):
            for low in range(4):
                rows = jnp.concatenate([t_ref[yy, low, xx, 0] for yy in range(4)], axis=0)
                high, rest_ = split(rows)
                at = (xx * 4 + low) * 32
                th_ref[at : at + 32, :] = high
                tl_ref[at : at + 32, :] = rest_

    rows = []
    for a in range(COLS // BLK):
        row = []
        for c in range(v_ref.shape[1] // BLK):
            weight = allowed_ref[step * (COLS // BLK) + a, c].astype(jnp.float32)
            row.append(v_ref[a * BLK : (a + 1) * BLK, c * BLK : (c + 1) * BLK] * weight)
        rows.append(jnp.concatenate(row, axis=1))
    vh, vl = split(jnp.concatenate(rows, axis=0))

    def dot(left, right):
        return lax.dot_general(left, right, NT, preferred_element_type=jnp.float32)

    th, tl = th_ref[...], tl_ref[...]
    total = dot(tl, vh) + dot(th, vl) + dot(th, vh)
    if got_ref is not None:
        total = total + got_ref[...]
    out_ref[...] = total


def ladder(par, allowed, amps, slab, got=None):
    width, depth = slab.shape
    in_specs = [
        pl.BlockSpec((4, 4, 4, 1, 8, depth), lambda i, par, allowed: (0, 0, 0, par[0], 0, 0)),
        pl.BlockSpec((COLS, depth), lambda i, par, allowed: (i, 0)),
    ]
    args = [amps, slab]
    if got is not None:
        in_specs.append(pl.BlockSpec((512, COLS), lambda i, par, allowed: (0, i)))
        args.append(got)
    return pl.pallas_call(
        ladder_body,
        out_shape=jax.ShapeDtypeStruct((512, width), jnp.float32),
        grid_spec=pltpu.PrefetchScalarGridSpec(
            num_scalar_prefetch=2,
            grid=(width // COLS,),
            in_specs=in_specs,
            out_specs=pl.BlockSpec((512, COLS), lambda i, par, allowed: (0, i)),
            scratch_shapes=[pltpu.VMEM((512, depth), jnp.bfloat16)] * 2,
        ),
        compiler_params=pltpu.CompilerParams(vmem_limit_bytes=32 * 2**20),
        cost_estimate=pl.CostEstimate(
            flops=6 * 512 * width * depth, bytes_accessed=8 * 2**20, transcendentals=0
        ),
    )(par, allowed, *args)


def everywhere(block, axes, size):
    spread = jnp.broadcast_to(block[None], (size, *block.shape))
    return lax.all_to_all(spread, axes, 0, 0)


def per_device(integrals, amplitudes, allowed):
    with jax.named_scope("gather_far"):
        far = everywhere(amplitudes, "zh", 8)
    with jax.named_scope("gather_near"):
        near = everywhere(far, "zl", 4)
    with jax.named_scope("gather_y"):
        amps = everywhere(near, "y", 4).reshape(4, 4, 4, 2, 8, 512)
    core = lax.axis_index("core").astype(jnp.int32)
    with jax.named_scope("other_half"):
        other = ladder((1 - core)[None], allowed, amps, integrals)
        got = lax.ppermute(other, "core", [(0, 1), (1, 0)])
    with jax.named_scope("own_half"):
        own = ladder(core[None], allowed, amps, integrals, got)
    with jax.named_scope("reduce_x"):
        parts = lax.all_to_all(own.reshape(4, 128, 1024), "x", 0, 0)
        return jnp.sum(parts, axis=0)


def solution(mesh):
    fine = Mesh(mesh.devices.reshape(8, 4, 4, 4, 2), ("zh", "zl", "y", "x", "core"))
    rows, cols = ("zh", "zl", "y"), ("x", "core")
    return jax.shard_map(
        per_device, mesh=fine, in_specs=(P(rows, cols),) * 3, out_specs=P(cols, rows), check_vma=False
    )
```

```python
import functools

import jax
import jax.numpy as jnp
from jax import lax
from jax.experimental import pallas as pl
from jax.experimental.pallas import tpu as pltpu
from jax.sharding import Mesh, PartitionSpec as P

BLK = 128
NT = (((1,), (1,)), ((), ()))
COLS = 256
PARAMS = pltpu.CompilerParams(vmem_limit_bytes=16 * 2**20)


def split(wide):
    high = wide.astype(jnp.bfloat16)
    return high, (wide - high.astype(jnp.float32)).astype(jnp.bfloat16)


def mask_body(allowed_ref, v_ref, kept_ref, high_ref, low_ref):
    step = pl.program_id(0)
    for a in range(COLS // BLK):
        rows = pl.ds(a * BLK, BLK)
        for c in range(v_ref.shape[1] // BLK):
            cols = pl.ds(c * BLK, BLK)
            weight = allowed_ref[step * (COLS // BLK) + a, c].astype(jnp.float32)
            kept = v_ref[rows, cols] * weight
            kept_ref[rows, cols] = kept
            high_ref[rows, cols], low_ref[rows, cols] = split(kept)


def masked(integrals, allowed):
    rows, depth = integrals.shape
    block = pl.BlockSpec((COLS, depth), lambda i, allowed: (i, 0))
    return pl.pallas_call(
        mask_body,
        out_shape=[jax.ShapeDtypeStruct((rows, depth), t) for t in (jnp.float32, jnp.bfloat16, jnp.bfloat16)],
        grid_spec=pltpu.PrefetchScalarGridSpec(
            num_scalar_prefetch=1, grid=(rows // COLS,), in_specs=[block], out_specs=[block] * 3
        ),
        compiler_params=PARAMS,
        cost_estimate=pl.CostEstimate(flops=2**21, bytes_accessed=6 * 2**20, transcendentals=0),
    )(allowed, integrals)


def parts_body(v_ref, high_ref, low_ref):
    high_ref[...], low_ref[...] = split(v_ref[...])


def parts_of(slab):
    rows, depth = slab.shape
    block = pl.BlockSpec((COLS, depth), lambda i: (i, 0))
    return pl.pallas_call(
        parts_body,
        out_shape=[jax.ShapeDtypeStruct((rows, depth), jnp.bfloat16)] * 2,
        grid=(rows // COLS,),
        in_specs=[block],
        out_specs=[block] * 2,
        compiler_params=PARAMS,
        cost_estimate=pl.CostEstimate(flops=2**21, bytes_accessed=4 * 2**20, transcendentals=0),
    )(slab)


def ladder_body(count, core_ref, *refs):
    t_refs, (oh_ref, ol_ref, sh_ref, sl_ref, out_ref, th_ref, tl_ref) = refs[:count], refs[count:]
    core = core_ref[0]
    size = 32 * count

    @pl.when(pl.program_id(0) == 0)
    def _():
        for side in range(2):
            source = core if side == 0 else 1 - core
            for xx in range(4):
                wide = jnp.concatenate([t[low, source, xx] for low in range(4) for t in t_refs], axis=0)
                at = pl.ds(xx * size, size)
                th_ref[side, at, :], tl_ref[side, at, :] = split(wide)

    def dot(left, right):
        return lax.dot_general(left, right, NT, preferred_element_type=jnp.float32)

    total = None
    for side, (vh_ref, vl_ref) in enumerate(((oh_ref, ol_ref), (sh_ref, sl_ref))):
        th, tl, vh = th_ref[side], tl_ref[side], vh_ref[...]
        term = dot(tl, vh) + dot(th, vl_ref[...]) + dot(th, vh)
        total = term if total is None else total + term
    out_ref[...] = total


def ladder(core, chunks, slabs):
    width, depth = slabs[0].shape
    rows = 128 * len(chunks)
    return pl.pallas_call(
        functools.partial(ladder_body, len(chunks)),
        out_shape=jax.ShapeDtypeStruct((rows, width), jnp.float32),
        grid_spec=pltpu.PrefetchScalarGridSpec(
            num_scalar_prefetch=1,
            grid=(width // COLS,),
            in_specs=[pl.BlockSpec((4, 2, 4, 8, depth), lambda i, core: (0, 0, 0, 0, 0))] * len(chunks)
            + [pl.BlockSpec((COLS, depth), lambda i, core: (i, 0))] * 4,
            out_specs=pl.BlockSpec((rows, COLS), lambda i, core: (0, i)),
            scratch_shapes=[pltpu.VMEM((2, rows, depth), jnp.bfloat16)] * 2,
        ),
        compiler_params=PARAMS,
        cost_estimate=pl.CostEstimate(
            flops=12 * rows * width * depth, bytes_accessed=4 * 2**20, transcendentals=0
        ),
    )(core, *chunks, *slabs)


def finish_body(y_ref, own_ref, sides_ref, across_ref, out_ref):
    me = y_ref[0]

    def put(offset, part_ref, k):
        place = lax.rem(me + offset, 4)
        for low in range(4):
            out_ref[low, place] = (part_ref[0, low, k] + part_ref[1, low, k]) + (part_ref[2, low, k] + part_ref[3, low, k])

    put(0, own_ref, 0)
    put(3, sides_ref, 0)
    put(1, sides_ref, 1)
    put(2, across_ref, 0)


def finish(y, own, sides, across):
    whole = lambda a: pl.BlockSpec(a.shape, lambda i, y: (0,) * a.ndim)
    out = jax.ShapeDtypeStruct((4, 4, 8, 1024), jnp.float32)
    return pl.pallas_call(
        finish_body,
        out_shape=out,
        grid_spec=pltpu.PrefetchScalarGridSpec(
            num_scalar_prefetch=1, grid=(1,), in_specs=[whole(a) for a in (own, sides, across)], out_specs=whole(out)
        ),
        compiler_params=PARAMS,
        cost_estimate=pl.CostEstimate(flops=2**19, bytes_accessed=5 * 2**19, transcendentals=0),
    )(y, own, sides, across)


def around(value, hops):
    return lax.ppermute(value, "y", [(i, (i + hops) % 4) for i in range(4)])


def over_x(partial):
    return lax.all_to_all(partial.reshape(4, 4, -1, 8, 1024), "x", 0, 0)


def per_device(integrals, amplitudes, allowed):
    core = lax.axis_index("core").astype(jnp.int32)[None]
    me = lax.axis_index("y").astype(jnp.int32)[None]
    with jax.named_scope("slab"):
        kept, own_high, own_low = masked(integrals, allowed)
        slabs = (own_high, own_low, *parts_of(lax.ppermute(kept, "core", [(0, 1), (1, 0)])))
    with jax.named_scope("gather_far"):
        far = lax.all_to_all(jnp.broadcast_to(amplitudes[None], (8, 8, 512)), "zh", 0, 0)
    with jax.named_scope("gather_near"):
        by_core = far.reshape(1, 4, 2, 8, 512).swapaxes(1, 2)
        spread = jnp.broadcast_to(by_core, (4, 2, 4, 8, 512)).reshape(8, 4, 8, 512)
        near = lax.all_to_all(spread, ("zl", "core"), 0, 0).reshape(4, 2, 4, 8, 512)
    with jax.named_scope("gather_y"):
        below, above = around(near, 1), around(near, 3)
        across = around(near, 2)
    with jax.named_scope("own_y"):
        own = over_x(ladder(core, [near], slabs))
    with jax.named_scope("sides_y"):
        sides = over_x(ladder(core, [below, above], slabs))
    with jax.named_scope("across_y"):
        opposite = over_x(ladder(core, [across], slabs))
    return finish(me, own, sides, opposite).reshape(128, 1024)


def solution(mesh):
    fine = Mesh(mesh.devices.reshape(8, 4, 4, 4, 2), ("zh", "zl", "y", "x", "core"))
    rows, cols = ("zh", "zl", "y"), ("x", "core")
    return jax.shard_map(
        per_device, mesh=fine, in_specs=(P(rows, cols),) * 3, out_specs=P(cols, rows), check_vma=False
    )
```

```python
import functools

import jax
import jax.numpy as jnp
from jax import lax
from jax.experimental import pallas as pl
from jax.experimental.pallas import tpu as pltpu
from jax.sharding import Mesh, PartitionSpec as P

BLK = 128
NT = (((1,), (1,)), ((), ()))
COLS = 256
PARAMS = pltpu.CompilerParams(vmem_limit_bytes=48 * 2**20)
COST = pl.CostEstimate(flops=1, bytes_accessed=1, transcendentals=0)


def split(wide):
    high = wide.astype(jnp.bfloat16)
    return high, (wide - high.astype(jnp.float32)).astype(jnp.bfloat16)


def mask_body(allowed_ref, v_ref, kept_ref):
    step = pl.program_id(0)
    for a in range(COLS // BLK):
        rows = pl.ds(a * BLK, BLK)
        for c in range(v_ref.shape[1] // BLK):
            cols = pl.ds(c * BLK, BLK)
            weight = allowed_ref[step * (COLS // BLK) + a, c].astype(jnp.float32)
            kept_ref[rows, cols] = v_ref[rows, cols] * weight


def masked(integrals, allowed):
    rows, depth = integrals.shape
    block = pl.BlockSpec((COLS, depth), lambda i, allowed: (i, 0))
    return pl.pallas_call(
        mask_body,
        out_shape=jax.ShapeDtypeStruct((rows, depth), jnp.float32),
        grid_spec=pltpu.PrefetchScalarGridSpec(
            num_scalar_prefetch=1, grid=(rows // COLS,), in_specs=[block], out_specs=block
        ),
        compiler_params=PARAMS,
        cost_estimate=COST,
    )(allowed, integrals)


def ladder_body(count, core_ref, *refs):
    t_refs, (own_ref, got_ref, out_ref, t_parts) = refs[:count], refs[count:]
    core = core_ref[0]
    size = 32 * count
    rows = 4 * size

    @pl.when(pl.program_id(0) == 0)
    def _():
        for side in range(2):
            source = core if side == 0 else 1 - core
            for xx in range(4):
                wide = jnp.concatenate([t[low, source, xx] for low in range(4) for t in t_refs], axis=0)
                high, low_part = split(wide)
                t_parts[side, pl.ds(xx * size, size), :] = high
                t_parts[side, pl.ds(rows + xx * size, size), :] = low_part

    def dot(left, right):
        return lax.dot_general(left, right, NT, preferred_element_type=jnp.float32)

    total = None
    for side, v_ref in enumerate((own_ref, got_ref)):
        high, low_part = split(v_ref[...])
        both = dot(t_parts[side], high)
        term = (both[rows:] + dot(t_parts[side, :rows], low_part)) + both[:rows]
        total = term if total is None else total + term
    out_ref[...] = total


def ladder(core, chunks, slabs):
    width, depth = slabs[0].shape
    rows = 128 * len(chunks)
    return pl.pallas_call(
        functools.partial(ladder_body, len(chunks)),
        out_shape=jax.ShapeDtypeStruct((rows, width), jnp.float32),
        grid_spec=pltpu.PrefetchScalarGridSpec(
            num_scalar_prefetch=1,
            grid=(width // COLS,),
            in_specs=[pl.BlockSpec((4, 2, 4, 8, depth), lambda i, core: (0, 0, 0, 0, 0))] * len(chunks)
            + [pl.BlockSpec((COLS, depth), lambda i, core: (i, 0))] * 2,
            out_specs=pl.BlockSpec((rows, COLS), lambda i, core: (0, i)),
            scratch_shapes=[pltpu.VMEM((2, 2 * rows, depth), jnp.bfloat16)],
        ),
        compiler_params=PARAMS,
        cost_estimate=COST,
    )(core, *chunks, *slabs)


def finish_body(y_ref, own_ref, sides_ref, across_ref, out_ref):
    me = y_ref[0]

    def put(offset, part_ref, k):
        place = lax.rem(me + offset, 4)
        out_ref[0, place] = (part_ref[0, 0, k] + part_ref[1, 0, k]) + (part_ref[2, 0, k] + part_ref[3, 0, k])

    put(0, own_ref, 0)
    put(3, sides_ref, 0)
    put(1, sides_ref, 1)
    put(2, across_ref, 0)


def finish(y, own, sides, across):
    def part(count):
        return pl.BlockSpec((4, 1, count, 8, 1024), lambda low, y: (0, low, 0, 0, 0))

    return pl.pallas_call(
        finish_body,
        out_shape=jax.ShapeDtypeStruct((4, 4, 8, 1024), jnp.float32),
        grid_spec=pltpu.PrefetchScalarGridSpec(
            num_scalar_prefetch=1,
            grid=(4,),
            in_specs=[part(1), part(2), part(1)],
            out_specs=pl.BlockSpec((1, 4, 8, 1024), lambda low, y: (low, 0, 0, 0)),
        ),
        compiler_params=PARAMS,
        cost_estimate=COST,
    )(y, own, sides, across)


def around(value, hops):
    return lax.ppermute(value, "y", [(i, (i + hops) % 4) for i in range(4)])


def over_x(partial):
    return lax.all_to_all(partial.reshape(4, 4, -1, 8, 1024), "x", 0, 0)


def per_device(integrals, amplitudes, allowed):
    core = lax.axis_index("core").astype(jnp.int32)[None]
    me = lax.axis_index("y").astype(jnp.int32)[None]
    with jax.named_scope("slab"):
        kept = masked(integrals, allowed)
        slabs = (kept, lax.ppermute(kept, "core", [(0, 1), (1, 0)]))
    with jax.named_scope("gather_far"):
        far = lax.all_to_all(jnp.broadcast_to(amplitudes[None], (8, 8, 512)), "zh", 0, 0)
    with jax.named_scope("gather_near"):
        by_core = far.reshape(1, 4, 2, 8, 512).swapaxes(1, 2)
        spread = jnp.broadcast_to(by_core, (4, 2, 4, 8, 512)).reshape(8, 4, 8, 512)
        near = lax.all_to_all(spread, ("zl", "core"), 0, 0).reshape(4, 2, 4, 8, 512)
    with jax.named_scope("gather_y"):
        below, above = around(near, 1), around(near, 3)
        across = around(near, 2)
    with jax.named_scope("own_y"):
        own = over_x(ladder(core, [near], slabs))
    with jax.named_scope("sides_y"):
        sides = over_x(ladder(core, [below, above], slabs))
    with jax.named_scope("across_y"):
        opposite = over_x(ladder(core, [across], slabs))
    return finish(me, own, sides, opposite).reshape(128, 1024)


def solution(mesh):
    fine = Mesh(mesh.devices.reshape(8, 4, 4, 4, 2), ("zh", "zl", "y", "x", "core"))
    rows, cols = ("zh", "zl", "y"), ("x", "core")
    return jax.shard_map(
        per_device, mesh=fine, in_specs=(P(rows, cols),) * 3, out_specs=P(cols, rows), check_vma=False
    )
```

```python
import functools

import jax
import jax.numpy as jnp
from jax import lax
from jax.experimental import pallas as pl
from jax.experimental.pallas import tpu as pltpu
from jax.sharding import Mesh, PartitionSpec as P

BLK = 128
NT = (((1,), (1,)), ((), ()))
COLS = 256
PARAMS = pltpu.CompilerParams(vmem_limit_bytes=48 * 2**20)
COST = pl.CostEstimate(flops=1, bytes_accessed=1, transcendentals=0)


def split(wide):
    high = wide.astype(jnp.bfloat16)
    return high, (wide - high.astype(jnp.float32)).astype(jnp.bfloat16)


def mask_body(allowed_ref, v_ref, kept_ref):
    step = pl.program_id(0)
    for a in range(COLS // BLK):
        rows = pl.ds(a * BLK, BLK)
        for c in range(v_ref.shape[1] // BLK):
            cols = pl.ds(c * BLK, BLK)
            weight = allowed_ref[step * (COLS // BLK) + a, c].astype(jnp.float32)
            kept_ref[rows, cols] = v_ref[rows, cols] * weight


def masked(integrals, allowed):
    rows, depth = integrals.shape
    block = pl.BlockSpec((COLS, depth), lambda i, allowed: (i, 0))
    return pl.pallas_call(
        mask_body,
        out_shape=jax.ShapeDtypeStruct((rows, depth), jnp.float32),
        grid_spec=pltpu.PrefetchScalarGridSpec(
            num_scalar_prefetch=1, grid=(rows // COLS,), in_specs=[block], out_specs=block
        ),
        compiler_params=PARAMS,
        cost_estimate=COST,
    )(allowed, integrals)


def ladder_body(count, core_ref, *refs):
    *t_refs, own_ref, got_ref, _, out_ref, t_parts = refs
    span = 4 * count // len(t_refs)
    core = core_ref[0]
    size = 32 * count
    rows = 4 * size

    @pl.when(pl.program_id(0) == 0)
    def _():
        for side in range(2):
            source = core if side == 0 else 1 - core
            for xx in range(4):
                rows_of = [
                    t_refs[y * (4 // span) + low // span][low % span, source, xx] for low in range(4) for y in range(count)
                ]
                wide = jnp.concatenate(rows_of, axis=0)
                high, low_part = split(wide)
                t_parts[side, pl.ds(xx * size, size), :] = high
                t_parts[side, pl.ds(rows + xx * size, size), :] = low_part

    def dot(left, right):
        return lax.dot_general(left, right, NT, preferred_element_type=jnp.float32)

    total = None
    for side, v_ref in enumerate((own_ref, got_ref)):
        high, low_part = split(v_ref[...])
        both = dot(t_parts[side], high)
        term = (both[rows:] + dot(t_parts[side, :rows], low_part)) + both[:rows]
        total = term if total is None else total + term
    out_ref[...] = total


def ladder(core, chunks, slabs, after):
    width, depth = slabs[0].shape
    span = chunks[0].shape[0]
    count = len(chunks) * span // 4
    rows = 128 * count
    return pl.pallas_call(
        functools.partial(ladder_body, count),
        out_shape=jax.ShapeDtypeStruct((rows, width), jnp.float32),
        grid_spec=pltpu.PrefetchScalarGridSpec(
            num_scalar_prefetch=1,
            grid=(width // COLS,),
            in_specs=[pl.BlockSpec((span, 2, 4, 8, depth), lambda i, core: (0, 0, 0, 0, 0))] * len(chunks)
            + [pl.BlockSpec((COLS, depth), lambda i, core: (i, 0))] * 2
            + [pl.BlockSpec(memory_space=pl.ANY)],
            out_specs=pl.BlockSpec((rows, COLS), lambda i, core: (0, i)),
            scratch_shapes=[pltpu.VMEM((2, 2 * rows, depth), jnp.bfloat16)],
        ),
        compiler_params=PARAMS,
        cost_estimate=COST,
    )(core, *chunks, *slabs, after)


def finish_body(y_ref, own_ref, sides_ref, across_ref, out_ref):
    me = y_ref[0]

    def put(offset, part_ref, k):
        place = lax.rem(me + offset, 4)
        out_ref[0, place] = (part_ref[0, 0, k] + part_ref[1, 0, k]) + (part_ref[2, 0, k] + part_ref[3, 0, k])

    put(0, own_ref, 0)
    put(3, sides_ref, 0)
    put(1, sides_ref, 1)
    put(2, across_ref, 0)


def finish(y, own, sides, across):
    def part(count):
        return pl.BlockSpec((4, 1, count, 8, 1024), lambda low, y: (0, low, 0, 0, 0))

    return pl.pallas_call(
        finish_body,
        out_shape=jax.ShapeDtypeStruct((4, 4, 8, 1024), jnp.float32),
        grid_spec=pltpu.PrefetchScalarGridSpec(
            num_scalar_prefetch=1,
            grid=(4,),
            in_specs=[part(1), part(2), part(1)],
            out_specs=pl.BlockSpec((1, 4, 8, 1024), lambda low, y: (low, 0, 0, 0)),
        ),
        compiler_params=PARAMS,
        cost_estimate=COST,
    )(y, own, sides, across)


def around(value, hops):
    return lax.ppermute(value, "y", [(i, (i + hops) % 4) for i in range(4)])


def over_x(partial):
    return lax.all_to_all(partial.reshape(4, 4, -1, 8, 1024), "x", 0, 0)


def per_device(integrals, amplitudes, allowed):
    core = lax.axis_index("core").astype(jnp.int32)[None]
    me = lax.axis_index("y").astype(jnp.int32)[None]
    with jax.named_scope("slab"):
        kept = masked(integrals, allowed)
        slabs = (kept, lax.ppermute(kept, "core", [(0, 1), (1, 0)]))
    with jax.named_scope("gather_far"):
        far = lax.all_to_all(jnp.broadcast_to(amplitudes[None], (8, 8, 512)), "zh", 0, 0)
    with jax.named_scope("gather_near"):
        by_core = far.reshape(1, 4, 2, 8, 512).swapaxes(1, 2)
        spread = jnp.broadcast_to(by_core, (4, 2, 4, 8, 512)).reshape(8, 4, 8, 512)
        near = lax.all_to_all(spread, ("zl", "core"), 0, 0).reshape(4, 2, 4, 8, 512)
    with jax.named_scope("gather_y"):
        below, above = around(near, 1), around(near, 3)
        across = [around(above[:2], 3), around(below[2:], 1)]
    with jax.named_scope("own_y"):
        own = ladder(core, [near], slabs, near)
    with jax.named_scope("sides_y"):
        sides = ladder(core, [below, above], slabs, own)
    with jax.named_scope("across_y"):
        opposite = ladder(core, across, slabs, sides)
    with jax.named_scope("reduce_x"):
        return finish(me, over_x(own), over_x(sides), over_x(opposite)).reshape(128, 1024)


def solution(mesh):
    fine = Mesh(mesh.devices.reshape(8, 4, 4, 4, 2), ("zh", "zl", "y", "x", "core"))
    rows, cols = ("zh", "zl", "y"), ("x", "core")
    return jax.shard_map(
        per_device, mesh=fine, in_specs=(P(rows, cols),) * 3, out_specs=P(cols, rows), check_vma=False
    )
```

```python
import functools

import jax
import jax.numpy as jnp
from jax import lax
from jax.experimental import pallas as pl
from jax.experimental.pallas import tpu as pltpu
from jax.sharding import Mesh, PartitionSpec as P

BLK = 128
NT = (((1,), (1,)), ((), ()))
COLS = 256
PARAMS = pltpu.CompilerParams(vmem_limit_bytes=48 * 2**20)
COST = pl.CostEstimate(flops=1, bytes_accessed=1, transcendentals=0)


def split(wide):
    high = wide.astype(jnp.bfloat16)
    return high, (wide - high.astype(jnp.float32)).astype(jnp.bfloat16)


def mask_body(allowed_ref, v_ref, kept_ref):
    step = pl.program_id(0)
    for a in range(COLS // BLK):
        rows = pl.ds(a * BLK, BLK)
        for c in range(v_ref.shape[1] // BLK):
            cols = pl.ds(c * BLK, BLK)
            weight = allowed_ref[step * (COLS // BLK) + a, c].astype(jnp.float32)
            kept_ref[rows, cols] = v_ref[rows, cols] * weight


def masked(integrals, allowed):
    rows, depth = integrals.shape
    block = pl.BlockSpec((COLS, depth), lambda i, allowed: (i, 0))
    return pl.pallas_call(
        mask_body,
        out_shape=jax.ShapeDtypeStruct((rows, depth), jnp.float32),
        grid_spec=pltpu.PrefetchScalarGridSpec(
            num_scalar_prefetch=1, grid=(rows // COLS,), in_specs=[block], out_specs=block
        ),
        compiler_params=PARAMS,
        cost_estimate=COST,
    )(allowed, integrals)


def ladder_body(count, core_ref, *refs):
    *t_refs, own_ref, got_ref, _, out_ref, t_parts = refs
    core = core_ref[0]
    size = 32 * count
    rows = 4 * size

    @pl.when(pl.program_id(0) == 0)
    def _():
        for side in range(2):
            source = core if side == 0 else 1 - core
            for xx in range(4):
                wide = jnp.concatenate([t[low, source, xx] for low in range(4) for t in t_refs], axis=0)
                high, low_part = split(wide)
                t_parts[side, pl.ds(xx * size, size), :] = high
                t_parts[side, pl.ds(rows + xx * size, size), :] = low_part

    def dot(left, right):
        return lax.dot_general(left, right, NT, preferred_element_type=jnp.float32)

    total = None
    for side, v_ref in enumerate((own_ref, got_ref)):
        high, low_part = split(v_ref[...])
        both = dot(t_parts[side], high)
        term = (both[rows:] + dot(t_parts[side, :rows], low_part)) + both[:rows]
        total = term if total is None else total + term
    out_ref[...] = total


def ladder(core, chunks, slabs, after):
    width, depth = slabs[0].shape
    count = len(chunks)
    rows = 128 * count
    return pl.pallas_call(
        functools.partial(ladder_body, count),
        out_shape=jax.ShapeDtypeStruct((rows, width), jnp.float32),
        grid_spec=pltpu.PrefetchScalarGridSpec(
            num_scalar_prefetch=1,
            grid=(width // COLS,),
            in_specs=[pl.BlockSpec((4, 2, 4, 8, depth), lambda i, core: (0, 0, 0, 0, 0))] * len(chunks)
            + [pl.BlockSpec((COLS, depth), lambda i, core: (i, 0))] * 2
            + [pl.BlockSpec(memory_space=pl.ANY)],
            out_specs=pl.BlockSpec((rows, COLS), lambda i, core: (0, i)),
            scratch_shapes=[pltpu.VMEM((2, 2 * rows, depth), jnp.bfloat16)],
        ),
        compiler_params=PARAMS,
        cost_estimate=pl.CostEstimate(flops=12 * rows * width * depth, bytes_accessed=16 * 2**20, transcendentals=0),
    )(core, *chunks, *slabs, after)


def finish_body(y_ref, own_ref, sides_ref, across_ref, out_ref):
    me = y_ref[0]

    def put(offset, part_ref, k):
        place = lax.rem(me + offset, 4)
        out_ref[0, place] = (part_ref[0, 0, k] + part_ref[1, 0, k]) + (part_ref[2, 0, k] + part_ref[3, 0, k])

    put(0, own_ref, 0)
    put(3, sides_ref, 0)
    put(1, sides_ref, 1)
    put(2, across_ref, 0)


def finish(y, own, sides, across):
    def part(count):
        return pl.BlockSpec((4, 1, count, 8, 1024), lambda low, y: (0, low, 0, 0, 0))

    return pl.pallas_call(
        finish_body,
        out_shape=jax.ShapeDtypeStruct((4, 4, 8, 1024), jnp.float32),
        grid_spec=pltpu.PrefetchScalarGridSpec(
            num_scalar_prefetch=1,
            grid=(4,),
            in_specs=[part(1), part(2), part(1)],
            out_specs=pl.BlockSpec((1, 4, 8, 1024), lambda low, y: (low, 0, 0, 0)),
        ),
        compiler_params=PARAMS,
        cost_estimate=COST,
    )(y, own, sides, across)


def around(value, hops):
    return lax.ppermute(value, "y", [(i, (i + hops) % 4) for i in range(4)])


def over_x(partial):
    return lax.all_to_all(partial.reshape(4, 4, -1, 8, 1024), "x", 0, 0)


def per_device(integrals, amplitudes, allowed):
    core = lax.axis_index("core").astype(jnp.int32)[None]
    me = lax.axis_index("y").astype(jnp.int32)[None]
    with jax.named_scope("slab"):
        kept = masked(integrals, allowed)
        slabs = (kept, lax.ppermute(kept, "core", [(0, 1), (1, 0)]))
    with jax.named_scope("gather_far"):
        far = lax.all_to_all(jnp.broadcast_to(amplitudes[None], (8, 8, 512)), "zh", 0, 0)
    with jax.named_scope("gather_near"):
        by_core = far.reshape(1, 4, 2, 8, 512).swapaxes(1, 2)
        spread = jnp.broadcast_to(by_core, (4, 2, 4, 8, 512)).reshape(8, 4, 8, 512)
        near = lax.all_to_all(spread, ("zl", "core"), 0, 0).reshape(4, 2, 4, 8, 512)
    with jax.named_scope("gather_y"):
        below, above = around(near, 1), around(near, 3)
        across = around(near, 2)
    with jax.named_scope("own_y"):
        own = ladder(core, [near], slabs, near)
    with jax.named_scope("sides_y"):
        sides = ladder(core, [below, above], slabs, own)
    with jax.named_scope("across_y"):
        opposite = ladder(core, [across], slabs, sides)
    with jax.named_scope("reduce_x"):
        return finish(me, over_x(own), over_x(sides), over_x(opposite)).reshape(128, 1024)


def solution(mesh):
    fine = Mesh(mesh.devices.reshape(8, 4, 4, 4, 2), ("zh", "zl", "y", "x", "core"))
    rows, cols = ("zh", "zl", "y"), ("x", "core")
    return jax.shard_map(
        per_device, mesh=fine, in_specs=(P(rows, cols),) * 3, out_specs=P(cols, rows), check_vma=False
    )
```

```python
import functools

import jax
import jax.numpy as jnp
from jax import lax
from jax.experimental import pallas as pl
from jax.experimental.pallas import tpu as pltpu
from jax.sharding import Mesh, PartitionSpec as P

BLK = 128
NT = (((1,), (1,)), ((), ()))
COLS = 256
PARAMS = pltpu.CompilerParams(vmem_limit_bytes=48 * 2**20)
COST = pl.CostEstimate(flops=1, bytes_accessed=1, transcendentals=0)


def split(wide):
    high = wide.astype(jnp.bfloat16)
    return high, (wide - high.astype(jnp.float32)).astype(jnp.bfloat16)


def mask_body(allowed_ref, v_ref, kept_ref):
    step = pl.program_id(0)
    for a in range(COLS // BLK):
        rows = pl.ds(a * BLK, BLK)
        for c in range(v_ref.shape[1] // BLK):
            cols = pl.ds(c * BLK, BLK)
            weight = allowed_ref[step * (COLS // BLK) + a, c].astype(jnp.float32)
            kept_ref[rows, cols] = v_ref[rows, cols] * weight


def masked(integrals, allowed):
    rows, depth = integrals.shape
    block = pl.BlockSpec((COLS, depth), lambda i, allowed: (i, 0))
    return pl.pallas_call(
        mask_body,
        out_shape=jax.ShapeDtypeStruct((rows, depth), jnp.float32),
        grid_spec=pltpu.PrefetchScalarGridSpec(
            num_scalar_prefetch=1, grid=(rows // COLS,), in_specs=[block], out_specs=block
        ),
        compiler_params=PARAMS,
        cost_estimate=COST,
    )(allowed, integrals)


def ladder_body(count, waits, where_ref, *refs):
    t_refs, (own_ref, got_ref) = refs[:count], refs[count : count + 2]
    out_refs, t_parts = refs[count + 2 + waits : -1], refs[-1]
    core, x = where_ref[0], where_ref[1]
    size = 32 * count
    rows = 4 * size

    @pl.when(pl.program_id(0) == 0)
    def _():
        for side in range(2):
            source = core if side == 0 else 1 - core
            for k in range(4):
                to = lax.rem(x + k, 4)
                wide = jnp.concatenate([t[low, source, to] for low in range(4) for t in t_refs], axis=0)
                high, low_part = split(wide)
                t_parts[side, pl.ds(k * size, size), :] = high
                t_parts[side, pl.ds(rows + k * size, size), :] = low_part
        if len(out_refs) > 4:
            out_refs[4][...] = t_refs[0][...]

    def dot(left, right):
        return lax.dot_general(left, right, NT, preferred_element_type=jnp.float32)

    total = None
    for side, v_ref in enumerate((own_ref, got_ref)):
        high, low_part = split(v_ref[...])
        both = dot(t_parts[side], high)
        term = (both[rows:] + dot(t_parts[side, :rows], low_part)) + both[:rows]
        total = term if total is None else total + term
    for k in range(4):
        out_refs[k][...] = total[k * size : (k + 1) * size]


def ladder(where, chunks, slabs, after=(), echo=False):
    width, depth = slabs[0].shape
    count = len(chunks)
    size = 32 * count
    whole = pl.BlockSpec((4, 2, 4, 8, depth), lambda i, where: (0, 0, 0, 0, 0))
    return pl.pallas_call(
        functools.partial(ladder_body, count, len(after)),
        out_shape=[jax.ShapeDtypeStruct((size, width), jnp.float32)] * 4
        + [jax.ShapeDtypeStruct(chunks[0].shape, jnp.float32)] * echo,
        grid_spec=pltpu.PrefetchScalarGridSpec(
            num_scalar_prefetch=1,
            grid=(width // COLS,),
            in_specs=[whole] * count
            + [pl.BlockSpec((COLS, depth), lambda i, where: (i, 0))] * 2
            + [pl.BlockSpec(memory_space=pl.ANY)] * len(after),
            out_specs=[pl.BlockSpec((size, COLS), lambda i, where: (0, i))] * 4 + [whole] * echo,
            scratch_shapes=[pltpu.VMEM((2, 8 * size, depth), jnp.bfloat16)],
        ),
        compiler_params=PARAMS,
        cost_estimate=pl.CostEstimate(
            flops=48 * size * width * depth, bytes_accessed=16 * 2**20, transcendentals=0
        ),
    )(where, *chunks, *slabs, *after)


def finish_body(y_ref, *refs):
    me = y_ref[0]
    own, sides, across, out_ref = refs[:4], refs[4:8], refs[8:12], refs[12]

    def put(offset, parts, k):
        a, b, c, d = (part[0, k] for part in parts)
        out_ref[0, lax.rem(me + offset, 4)] = (a + b) + (c + d)

    put(0, own, 0)
    put(3, sides, 0)
    put(1, sides, 1)
    put(2, across, 0)


def finish(y, *chunks):
    parts = [part.reshape(4, -1, 8, 1024) for chunk in chunks for part in chunk]
    return pl.pallas_call(
        finish_body,
        out_shape=jax.ShapeDtypeStruct((4, 4, 8, 1024), jnp.float32),
        grid_spec=pltpu.PrefetchScalarGridSpec(
            num_scalar_prefetch=1,
            grid=(4,),
            in_specs=[pl.BlockSpec((1, *part.shape[1:]), lambda low, y: (low, 0, 0, 0)) for part in parts],
            out_specs=pl.BlockSpec((1, 4, 8, 1024), lambda low, y: (low, 0, 0, 0)),
        ),
        compiler_params=PARAMS,
        cost_estimate=COST,
    )(y, *parts)


def shift(value, axis, hops):
    return lax.ppermute(value, axis, [(i, (i + hops) % 4) for i in range(4)])


def over_x(parts):
    return [parts[0]] + [shift(parts[k], "x", k) for k in (2, 1, 3)]


def per_device(integrals, amplitudes, allowed):
    core, x, y = (lax.axis_index(axis).astype(jnp.int32) for axis in ("core", "x", "y"))
    where = jnp.stack([core, x])
    with jax.named_scope("slab"):
        kept = masked(integrals, allowed)
        slabs = (kept, lax.ppermute(kept, "core", [(0, 1), (1, 0)]))
    with jax.named_scope("gather_far"):
        far = lax.all_to_all(jnp.broadcast_to(amplitudes[None], (8, 8, 512)), "zh", 0, 0)
    with jax.named_scope("gather_near"):
        by_core = far.reshape(1, 4, 2, 8, 512).swapaxes(1, 2)
        spread = jnp.broadcast_to(by_core, (4, 2, 4, 8, 512)).reshape(8, 4, 8, 512)
        near = lax.all_to_all(spread, ("zl", "core"), 0, 0).reshape(4, 2, 4, 8, 512)
    with jax.named_scope("gather_sides"):
        below, above = shift(near, "y", 1), shift(near, "y", 3)
    with jax.named_scope("own_y"):
        *own, echo = ladder(where, [near], slabs, echo=True)
        own_sums = over_x(own)
    with jax.named_scope("gather_across"):
        across = shift(echo, "y", 2)
    with jax.named_scope("sides_y"):
        sides = ladder(where, [below, above], slabs, [own[0]])
        sides_sums = over_x(sides)
    with jax.named_scope("across_y"):
        opposite = ladder(where, [across], slabs, [sides[0], *own_sums[1:]])
        across_sums = over_x(opposite)
    with jax.named_scope("finish"):
        return finish(y[None], own_sums, sides_sums, across_sums).reshape(128, 1024)


def solution(mesh):
    fine = Mesh(mesh.devices.reshape(8, 4, 4, 4, 2), ("zh", "zl", "y", "x", "core"))
    rows, cols = ("zh", "zl", "y"), ("x", "core")
    return jax.shard_map(
        per_device, mesh=fine, in_specs=(P(rows, cols),) * 3, out_specs=P(cols, rows), check_vma=False
    )
```

```python
import functools

import jax
import jax.numpy as jnp
from jax import lax
from jax.experimental import pallas as pl
from jax.experimental.pallas import tpu as pltpu
from jax.sharding import Mesh, PartitionSpec as P

BLK = 128
NT = (((1,), (1,)), ((), ()))
COLS = 256
PARAMS = pltpu.CompilerParams(vmem_limit_bytes=48 * 2**20)
COST = pl.CostEstimate(flops=1, bytes_accessed=1, transcendentals=0)


def split(wide):
    high = wide.astype(jnp.bfloat16)
    return high, (wide - high.astype(jnp.float32)).astype(jnp.bfloat16)


def mask_body(allowed_ref, v_ref, kept_ref):
    step = pl.program_id(0)
    for a in range(COLS // BLK):
        rows = pl.ds(a * BLK, BLK)
        for c in range(v_ref.shape[1] // BLK):
            cols = pl.ds(c * BLK, BLK)
            weight = allowed_ref[step * (COLS // BLK) + a, c].astype(jnp.float32)
            kept_ref[rows, cols] = v_ref[rows, cols] * weight


def masked(integrals, allowed):
    rows, depth = integrals.shape
    block = pl.BlockSpec((COLS, depth), lambda i, allowed: (i, 0))
    return pl.pallas_call(
        mask_body,
        out_shape=jax.ShapeDtypeStruct((rows, depth), jnp.float32),
        grid_spec=pltpu.PrefetchScalarGridSpec(
            num_scalar_prefetch=1, grid=(rows // COLS,), in_specs=[block], out_specs=block
        ),
        compiler_params=PARAMS,
        cost_estimate=COST,
    )(allowed, integrals)


def ladder_body(count, core_ref, *refs):
    t_hbm, (own_hbm, got_hbm, out_hbm) = refs[:count], refs[count : count + 3]
    t_buf, v_buf, o_buf, t_parts, t_sem, v_sem, o_sem = refs[count + 3 :]
    core = core_ref[0]
    size = 32 * count
    rows = 4 * size
    blocks = own_hbm.shape[0] // COLS

    t_copies = [pltpu.make_async_copy(t_hbm[y], t_buf.at[y], t_sem.at[y]) for y in range(count)]
    for copy in t_copies:
        copy.start()
    v_copies = []
    for j in range(blocks):
        for side, v_hbm in enumerate((own_hbm, got_hbm)):
            at = pl.ds(j * COLS, COLS)
            copy = pltpu.make_async_copy(v_hbm.at[at, :], v_buf.at[side, at, :], v_sem.at[j, side])
            copy.start()
            v_copies.append(copy)

    for copy in t_copies:
        copy.wait()
    for side in range(2):
        source = core if side == 0 else 1 - core
        for xx in range(4):
            wide = jnp.concatenate([t_buf[y, low, source, xx] for low in range(4) for y in range(count)], axis=0)
            high, low_part = split(wide)
            t_parts[side, pl.ds(xx * size, size), :] = high
            t_parts[side, pl.ds(rows + xx * size, size), :] = low_part

    def dot(left, right):
        return lax.dot_general(left, right, NT, preferred_element_type=jnp.float32)

    o_copies = []
    for j in range(blocks):
        at = pl.ds(j * COLS, COLS)
        total = None
        for side in range(2):
            v_copies[2 * j + side].wait()
            high, low_part = split(v_buf[side, at, :])
            both = dot(t_parts[side], high)
            term = (both[rows:] + dot(t_parts[side, :rows], low_part)) + both[:rows]
            total = term if total is None else total + term
        o_buf[:, at] = total
        copy = pltpu.make_async_copy(o_buf.at[:, at], out_hbm.at[:, at], o_sem.at[j])
        copy.start()
        o_copies.append(copy)
    for copy in o_copies:
        copy.wait()


def ladder(core, chunks, slabs):
    width, depth = slabs[0].shape
    count = len(chunks)
    rows = 128 * count
    blocks = width // COLS
    hbm = pl.BlockSpec(memory_space=pltpu.HBM)
    return pl.pallas_call(
        functools.partial(ladder_body, count),
        out_shape=jax.ShapeDtypeStruct((rows, width), jnp.float32),
        in_specs=[pl.BlockSpec(memory_space=pltpu.SMEM)] + [hbm] * (count + 2),
        out_specs=hbm,
        scratch_shapes=[
            pltpu.VMEM((count, 4, 2, 4, 8, depth), jnp.float32),
            pltpu.VMEM((2, width, depth), jnp.float32),
            pltpu.VMEM((rows, width), jnp.float32),
            pltpu.VMEM((2, 2 * rows, depth), jnp.bfloat16),
            pltpu.SemaphoreType.DMA((count,)),
            pltpu.SemaphoreType.DMA((blocks, 2)),
            pltpu.SemaphoreType.DMA((blocks,)),
        ],
        compiler_params=PARAMS,
        cost_estimate=COST,
    )(core, *chunks, *slabs)


def finish_body(y_ref, own_ref, sides_ref, across_ref, out_ref):
    me = y_ref[0]

    def put(offset, part_ref, k):
        place = lax.rem(me + offset, 4)
        out_ref[0, place] = (part_ref[0, 0, k] + part_ref[1, 0, k]) + (part_ref[2, 0, k] + part_ref[3, 0, k])

    put(0, own_ref, 0)
    put(3, sides_ref, 0)
    put(1, sides_ref, 1)
    put(2, across_ref, 0)


def finish(y, own, sides, across):
    def part(count):
        return pl.BlockSpec((4, 1, count, 8, 1024), lambda low, y: (0, low, 0, 0, 0))

    return pl.pallas_call(
        finish_body,
        out_shape=jax.ShapeDtypeStruct((4, 4, 8, 1024), jnp.float32),
        grid_spec=pltpu.PrefetchScalarGridSpec(
            num_scalar_prefetch=1,
            grid=(4,),
            in_specs=[part(1), part(2), part(1)],
            out_specs=pl.BlockSpec((1, 4, 8, 1024), lambda low, y: (low, 0, 0, 0)),
        ),
        compiler_params=PARAMS,
        cost_estimate=COST,
    )(y, own, sides, across)


def around(value, hops):
    return lax.ppermute(value, "y", [(i, (i + hops) % 4) for i in range(4)])


def over_x(partial):
    return lax.all_to_all(partial.reshape(4, 4, -1, 8, 1024), "x", 0, 0)


def per_device(integrals, amplitudes, allowed):
    core = lax.axis_index("core").astype(jnp.int32)[None]
    me = lax.axis_index("y").astype(jnp.int32)[None]
    with jax.named_scope("slab"):
        kept = masked(integrals, allowed)
        slabs = (kept, lax.ppermute(kept, "core", [(0, 1), (1, 0)]))
    with jax.named_scope("gather_far"):
        far = lax.all_to_all(jnp.broadcast_to(amplitudes[None], (8, 8, 512)), "zh", 0, 0)
    with jax.named_scope("gather_near"):
        by_core = far.reshape(1, 4, 2, 8, 512).swapaxes(1, 2)
        spread = jnp.broadcast_to(by_core, (4, 2, 4, 8, 512)).reshape(8, 4, 8, 512)
        near = lax.all_to_all(spread, ("zl", "core"), 0, 0).reshape(4, 2, 4, 8, 512)
    with jax.named_scope("gather_y"):
        below, above = around(near, 1), around(near, 3)
        across = around(near, 2)
    with jax.named_scope("own_y"):
        own = over_x(ladder(core, [near], slabs))
    with jax.named_scope("sides_y"):
        sides = over_x(ladder(core, [below, above], slabs))
    with jax.named_scope("across_y"):
        opposite = over_x(ladder(core, [across], slabs))
    return finish(me, own, sides, opposite).reshape(128, 1024)


def solution(mesh):
    fine = Mesh(mesh.devices.reshape(8, 4, 4, 4, 2), ("zh", "zl", "y", "x", "core"))
    rows, cols = ("zh", "zl", "y"), ("x", "core")
    return jax.shard_map(
        per_device, mesh=fine, in_specs=(P(rows, cols),) * 3, out_specs=P(cols, rows), check_vma=False
    )
```

```python
import functools

import jax
import jax.numpy as jnp
from jax import lax
from jax.experimental import pallas as pl
from jax.experimental.pallas import tpu as pltpu
from jax.sharding import Mesh, PartitionSpec as P

BLK = 128
NT = (((1,), (1,)), ((), ()))
COLS = 256
PARAMS = pltpu.CompilerParams(vmem_limit_bytes=48 * 2**20)
COST = pl.CostEstimate(flops=1, bytes_accessed=1, transcendentals=0)


def split(wide):
    high = wide.astype(jnp.bfloat16)
    return high, (wide - high.astype(jnp.float32)).astype(jnp.bfloat16)


def mask_body(allowed_ref, v_ref, kept_ref, high_ref, low_ref):
    step = pl.program_id(0)
    for a in range(COLS // BLK):
        rows = pl.ds(a * BLK, BLK)
        for c in range(v_ref.shape[1] // BLK):
            cols = pl.ds(c * BLK, BLK)
            weight = allowed_ref[step * (COLS // BLK) + a, c].astype(jnp.float32)
            kept = v_ref[rows, cols] * weight
            kept_ref[rows, cols] = kept
            high_ref[rows, cols], low_ref[rows, cols] = split(kept)


def masked(integrals, allowed):
    rows, depth = integrals.shape
    block = pl.BlockSpec((COLS, depth), lambda i, allowed: (i, 0))
    return pl.pallas_call(
        mask_body,
        out_shape=[jax.ShapeDtypeStruct((rows, depth), t) for t in (jnp.float32, jnp.bfloat16, jnp.bfloat16)],
        grid_spec=pltpu.PrefetchScalarGridSpec(
            num_scalar_prefetch=1, grid=(rows // COLS,), in_specs=[block], out_specs=[block] * 3
        ),
        compiler_params=PARAMS,
        cost_estimate=COST,
    )(allowed, integrals)


def ladder_body(count, first, core_ref, *refs):
    t_hbm, (own_high, own_low), refs = refs[:count], refs[count : count + 2], refs[count + 2 :]
    if first:
        got_hbm, out_hbm, got_high, got_low, *refs = refs
    else:
        got_high, got_low, out_hbm, *refs = refs
    t_buf, high_buf, low_buf, o_buf, t_parts, t_sem, v_sem, o_sem, *rest = refs
    core = core_ref[0]
    size = 32 * count
    rows = 4 * size
    width, depth = own_high.shape
    blocks = width // COLS
    near_cols, far_cols = pl.ds(0, depth), pl.ds(depth, depth)

    def started(source, target, sem):
        copy = pltpu.make_async_copy(source, target, sem)
        copy.start()
        return copy

    t_copies = [started(t_hbm[y], t_buf.at[y], t_sem.at[y]) for y in range(count)]
    v_copies = []
    for j in range(blocks):
        at = pl.ds(j * COLS, COLS)
        block = [
            started(own_high.at[at, :], high_buf.at[at, near_cols], v_sem.at[j, 0]),
            started(own_low.at[at, :], low_buf.at[at, near_cols], v_sem.at[j, 1]),
        ]
        if first:
            block.append(started(got_hbm.at[at, :], rest[0].at[at, :], v_sem.at[j, 2]))
        else:
            block.append(started(got_high.at[at, :], high_buf.at[at, far_cols], v_sem.at[j, 2]))
            block.append(started(got_low.at[at, :], low_buf.at[at, far_cols], v_sem.at[j, 3]))
        v_copies.append(block)

    for copy in t_copies:
        copy.wait()
    for side, cols in enumerate((near_cols, far_cols)):
        source = core if side == 0 else 1 - core
        for xx in range(4):
            wide = jnp.concatenate([t_buf[y, low, source, xx] for low in range(4) for y in range(count)], axis=0)
            high, low_part = split(wide)
            t_parts[pl.ds(xx * size, size), cols] = high
            t_parts[pl.ds(rows + xx * size, size), cols] = low_part

    def dot(left, right):
        return lax.dot_general(left, right, NT, preferred_element_type=jnp.float32)

    o_copies = []
    for j in range(blocks):
        at = pl.ds(j * COLS, COLS)
        for copy in v_copies[j]:
            copy.wait()
        if first:
            high_buf[at, far_cols], low_buf[at, far_cols] = split(rest[0][at, :])
            o_copies.append(started(high_buf.at[at, far_cols], got_high.at[at, :], rest[1].at[j, 0]))
            o_copies.append(started(low_buf.at[at, far_cols], got_low.at[at, :], rest[1].at[j, 1]))
        both = dot(t_parts[...], high_buf[at, :])
        o_buf[:, at] = (both[rows:] + dot(t_parts[:rows, :], low_buf[at, :])) + both[:rows]
        o_copies.append(started(o_buf.at[:, at], out_hbm.at[:, at], o_sem.at[j]))
    for copy in o_copies:
        copy.wait()


def ladder(core, chunks, own_parts, got):
    width, depth = own_parts[0].shape
    first = len(got) == 1
    count = len(chunks)
    rows = 128 * count
    blocks = width // COLS
    hbm = pl.BlockSpec(memory_space=pltpu.HBM)
    part = jax.ShapeDtypeStruct((width, depth), jnp.bfloat16)
    return pl.pallas_call(
        functools.partial(ladder_body, count, first),
        out_shape=[jax.ShapeDtypeStruct((rows, width), jnp.float32)] + [part] * (2 * first),
        in_specs=[pl.BlockSpec(memory_space=pltpu.SMEM)] + [hbm] * (count + 2 + len(got)),
        out_specs=[hbm] * (1 + 2 * first),
        scratch_shapes=[
            pltpu.VMEM((count, 4, 2, 4, 8, depth), jnp.float32),
            pltpu.VMEM((width, 2 * depth), jnp.bfloat16),
            pltpu.VMEM((width, 2 * depth), jnp.bfloat16),
            pltpu.VMEM((rows, width), jnp.float32),
            pltpu.VMEM((2 * rows, 2 * depth), jnp.bfloat16),
            pltpu.SemaphoreType.DMA((count,)),
            pltpu.SemaphoreType.DMA((blocks, 4)),
            pltpu.SemaphoreType.DMA((blocks,)),
        ]
        + [pltpu.VMEM((width, depth), jnp.float32), pltpu.SemaphoreType.DMA((blocks, 2))] * first,
        compiler_params=PARAMS,
        cost_estimate=COST,
    )(core, *chunks, *own_parts, *got)


def finish_body(y_ref, own_ref, sides_ref, across_ref, out_ref):
    me = y_ref[0]

    def put(offset, part_ref, k):
        place = lax.rem(me + offset, 4)
        out_ref[0, place] = (part_ref[0, 0, k] + part_ref[1, 0, k]) + (part_ref[2, 0, k] + part_ref[3, 0, k])

    put(0, own_ref, 0)
    put(3, sides_ref, 0)
    put(1, sides_ref, 1)
    put(2, across_ref, 0)


def finish(y, own, sides, across):
    def part(count):
        return pl.BlockSpec((4, 1, count, 8, 1024), lambda low, y: (0, low, 0, 0, 0))

    return pl.pallas_call(
        finish_body,
        out_shape=jax.ShapeDtypeStruct((4, 4, 8, 1024), jnp.float32),
        grid_spec=pltpu.PrefetchScalarGridSpec(
            num_scalar_prefetch=1,
            grid=(4,),
            in_specs=[part(1), part(2), part(1)],
            out_specs=pl.BlockSpec((1, 4, 8, 1024), lambda low, y: (low, 0, 0, 0)),
        ),
        compiler_params=PARAMS,
        cost_estimate=COST,
    )(y, own, sides, across)


def around(value, hops):
    return lax.ppermute(value, "y", [(i, (i + hops) % 4) for i in range(4)])


def over_x(partial):
    return lax.all_to_all(partial.reshape(4, 4, -1, 8, 1024), "x", 0, 0)


def per_device(integrals, amplitudes, allowed):
    core = lax.axis_index("core").astype(jnp.int32)[None]
    me = lax.axis_index("y").astype(jnp.int32)[None]
    with jax.named_scope("slab"):
        kept, *own_parts = masked(integrals, allowed)
        got = lax.ppermute(kept, "core", [(0, 1), (1, 0)])
    with jax.named_scope("gather_far"):
        far = lax.all_to_all(jnp.broadcast_to(amplitudes[None], (8, 8, 512)), "zh", 0, 0)
    with jax.named_scope("gather_near"):
        by_core = far.reshape(1, 4, 2, 8, 512).swapaxes(1, 2)
        spread = jnp.broadcast_to(by_core, (4, 2, 4, 8, 512)).reshape(8, 4, 8, 512)
        near = lax.all_to_all(spread, ("zl", "core"), 0, 0).reshape(4, 2, 4, 8, 512)
    with jax.named_scope("gather_y"):
        below, above = around(near, 1), around(near, 3)
        across = around(near, 2)
    with jax.named_scope("own_y"):
        own, *got_parts = ladder(core, [near], own_parts, [got])
        own = over_x(own)
    with jax.named_scope("sides_y"):
        sides = over_x(*ladder(core, [below, above], own_parts, got_parts))
    with jax.named_scope("across_y"):
        opposite = over_x(*ladder(core, [across], own_parts, got_parts))
    return finish(me, own, sides, opposite).reshape(128, 1024)


def solution(mesh):
    fine = Mesh(mesh.devices.reshape(8, 4, 4, 4, 2), ("zh", "zl", "y", "x", "core"))
    rows, cols = ("zh", "zl", "y"), ("x", "core")
    return jax.shard_map(
        per_device, mesh=fine, in_specs=(P(rows, cols),) * 3, out_specs=P(cols, rows), check_vma=False
    )
```

```python
import functools

import jax
import jax.numpy as jnp
from jax import lax
from jax.experimental import pallas as pl
from jax.experimental.pallas import tpu as pltpu
from jax.sharding import Mesh, PartitionSpec as P

BLK = 128
NT = (((1,), (1,)), ((), ()))
COLS = 256
PARAMS = pltpu.CompilerParams(vmem_limit_bytes=48 * 2**20)
COST = pl.CostEstimate(flops=1, bytes_accessed=1, transcendentals=0)


def split(wide):
    high = wide.astype(jnp.bfloat16)
    return high, (wide - high.astype(jnp.float32)).astype(jnp.bfloat16)


def mask_body(allowed_ref, v_ref, kept_ref):
    step = pl.program_id(0)
    for a in range(COLS // BLK):
        rows = pl.ds(a * BLK, BLK)
        for c in range(v_ref.shape[1] // BLK):
            cols = pl.ds(c * BLK, BLK)
            weight = allowed_ref[step * (COLS // BLK) + a, c].astype(jnp.float32)
            kept_ref[rows, cols] = v_ref[rows, cols] * weight


def masked(integrals, allowed):
    rows, depth = integrals.shape
    block = pl.BlockSpec((COLS, depth), lambda i, allowed: (i, 0))
    return pl.pallas_call(
        mask_body,
        out_shape=jax.ShapeDtypeStruct((rows, depth), jnp.float32),
        grid_spec=pltpu.PrefetchScalarGridSpec(
            num_scalar_prefetch=1, grid=(rows // COLS,), in_specs=[block], out_specs=block
        ),
        compiler_params=PARAMS,
        cost_estimate=COST,
    )(allowed, integrals)


def ladder_body(count, core_ref, *refs):
    t_refs, (own_ref, got_ref, out_ref, t_parts) = refs[:count], refs[count:]
    core = core_ref[0]
    size = 32 * count
    rows = 4 * size

    @pl.when(pl.program_id(0) == 0)
    def _():
        for side in range(2):
            source = core if side == 0 else 1 - core
            for xx in range(4):
                wide = jnp.concatenate([t[low, source, xx] for low in range(4) for t in t_refs], axis=0)
                high, low_part = split(wide)
                t_parts[side, pl.ds(xx * size, size), :] = high
                t_parts[side, pl.ds(rows + xx * size, size), :] = low_part

    def dot(left, right):
        return lax.dot_general(left, right, NT, preferred_element_type=jnp.float32)

    total = None
    for side, v_ref in enumerate((own_ref, got_ref)):
        high, low_part = split(v_ref[...])
        both = dot(t_parts[side], high)
        term = (both[rows:] + dot(t_parts[side, :rows], low_part)) + both[:rows]
        total = term if total is None else total + term
    out_ref[...] = total


def ladder(core, chunks, slabs):
    width, depth = slabs[0].shape
    rows = 128 * len(chunks)
    return pl.pallas_call(
        functools.partial(ladder_body, len(chunks)),
        out_shape=jax.ShapeDtypeStruct((rows, width), jnp.float32),
        grid_spec=pltpu.PrefetchScalarGridSpec(
            num_scalar_prefetch=1,
            grid=(width // COLS,),
            in_specs=[pl.BlockSpec((4, 2, 4, 8, depth), lambda i, core: (0, 0, 0, 0, 0))] * len(chunks)
            + [pl.BlockSpec((COLS, depth), lambda i, core: (i, 0))] * 2,
            out_specs=pl.BlockSpec((rows, COLS), lambda i, core: (0, i)),
            scratch_shapes=[pltpu.VMEM((2, 2 * rows, depth), jnp.bfloat16)],
        ),
        compiler_params=PARAMS,
        cost_estimate=COST,
    )(core, *chunks, *slabs)


def finish_body(y_ref, own_ref, sides_ref, across_ref, out_ref):
    me = y_ref[0]

    def put(offset, part_ref, k):
        place = lax.rem(me + offset, 4)
        out_ref[0, place] = (part_ref[0, 0, k] + part_ref[1, 0, k]) + (part_ref[2, 0, k] + part_ref[3, 0, k])

    put(0, own_ref, 0)
    put(3, sides_ref, 0)
    put(1, sides_ref, 1)
    put(2, across_ref, 0)


def finish(y, own, sides, across):
    def part(count):
        return pl.BlockSpec((4, 1, count, 8, 1024), lambda low, y: (0, low, 0, 0, 0))

    return pl.pallas_call(
        finish_body,
        out_shape=jax.ShapeDtypeStruct((4, 4, 8, 1024), jnp.float32),
        grid_spec=pltpu.PrefetchScalarGridSpec(
            num_scalar_prefetch=1,
            grid=(4,),
            in_specs=[part(1), part(2), part(1)],
            out_specs=pl.BlockSpec((1, 4, 8, 1024), lambda low, y: (low, 0, 0, 0)),
        ),
        compiler_params=PARAMS,
        cost_estimate=COST,
    )(y, own, sides, across)


def around(value, hops):
    return lax.ppermute(value, "y", [(i, (i + hops) % 4) for i in range(4)])


def over_x(partial):
    return lax.all_to_all(partial.reshape(4, 4, -1, 8, 1024), "x", 0, 0)


def per_device(integrals, amplitudes, allowed):
    core = lax.axis_index("core").astype(jnp.int32)[None]
    me = lax.axis_index("y").astype(jnp.int32)[None]
    with jax.named_scope("slab"):
        kept = masked(integrals, allowed)
        slabs = (kept, lax.ppermute(kept, "core", [(0, 1), (1, 0)]))
    with jax.named_scope("gather_far"):
        far = lax.all_gather(amplitudes, "zh")
    with jax.named_scope("gather_near"):
        by_core = far.reshape(1, 4, 2, 8, 512).swapaxes(1, 2)
        spread = jnp.broadcast_to(by_core, (4, 2, 4, 8, 512)).reshape(8, 4, 8, 512)
        near = lax.all_to_all(spread, ("zl", "core"), 0, 0).reshape(4, 2, 4, 8, 512)
    with jax.named_scope("gather_y"):
        below, above = around(near, 1), around(near, 3)
        across = around(near, 2)
    with jax.named_scope("own_y"):
        own = over_x(ladder(core, [near], slabs))
    with jax.named_scope("sides_y"):
        sides = over_x(ladder(core, [below, above], slabs))
    with jax.named_scope("across_y"):
        opposite = over_x(ladder(core, [across], slabs))
    return finish(me, own, sides, opposite).reshape(128, 1024)


def solution(mesh):
    fine = Mesh(mesh.devices.reshape(8, 4, 4, 4, 2), ("zh", "zl", "y", "x", "core"))
    rows, cols = ("zh", "zl", "y"), ("x", "core")
    return jax.shard_map(
        per_device, mesh=fine, in_specs=(P(rows, cols),) * 3, out_specs=P(cols, rows), check_vma=False
    )
```

```python
import functools

import jax
import jax.numpy as jnp
from jax import lax
from jax.experimental import pallas as pl
from jax.experimental.pallas import tpu as pltpu
from jax.sharding import Mesh, PartitionSpec as P

BLK = 128
NT = (((1,), (1,)), ((), ()))
COLS = 256
WIDE = 512
PARAMS = pltpu.CompilerParams(vmem_limit_bytes=48 * 2**20)
COST = pl.CostEstimate(flops=1, bytes_accessed=1, transcendentals=0)


def split(wide):
    high = wide.astype(jnp.bfloat16)
    return high, (wide - high.astype(jnp.float32)).astype(jnp.bfloat16)


def mask_body(allowed_ref, v_ref, kept_ref):
    step = pl.program_id(0)
    for a in range(COLS // BLK):
        rows = pl.ds(a * BLK, BLK)
        for c in range(v_ref.shape[1] // BLK):
            cols = pl.ds(c * BLK, BLK)
            weight = allowed_ref[step * (COLS // BLK) + a, c].astype(jnp.float32)
            kept_ref[rows, cols] = v_ref[rows, cols] * weight


def masked(integrals, allowed):
    rows, depth = integrals.shape
    block = pl.BlockSpec((COLS, depth), lambda i, allowed: (i, 0))
    return pl.pallas_call(
        mask_body,
        out_shape=jax.ShapeDtypeStruct((rows, depth), jnp.float32),
        grid_spec=pltpu.PrefetchScalarGridSpec(
            num_scalar_prefetch=1, grid=(rows // COLS,), in_specs=[block], out_specs=block
        ),
        compiler_params=PARAMS,
        cost_estimate=COST,
    )(allowed, integrals)


def ladder_body(count, core_ref, *refs):
    t_refs, (own_ref, got_ref, out_ref, t_parts) = refs[:count], refs[count:]
    core = core_ref[0]
    size = 32 * count
    rows = 4 * size

    @pl.when(pl.program_id(0) == 0)
    def _():
        for side in range(2):
            source = core if side == 0 else 1 - core
            for xx in range(4):
                wide = jnp.concatenate([t[low, source, xx] for low in range(4) for t in t_refs], axis=0)
                high, low_part = split(wide)
                t_parts[side, pl.ds(xx * size, size), :] = high
                t_parts[side, pl.ds(rows + xx * size, size), :] = low_part

    def dot(left, right):
        return lax.dot_general(left, right, NT, preferred_element_type=jnp.float32)

    total = None
    for side, v_ref in enumerate((own_ref, got_ref)):
        high, low_part = split(v_ref[...])
        both = dot(t_parts[side], high)
        term = (both[rows:] + dot(t_parts[side, :rows], low_part)) + both[:rows]
        total = term if total is None else total + term
    out_ref[...] = total


def ladder(core, chunks, slabs):
    width, depth = slabs[0].shape
    rows = 128 * len(chunks)
    return pl.pallas_call(
        functools.partial(ladder_body, len(chunks)),
        out_shape=jax.ShapeDtypeStruct((rows, width), jnp.float32),
        grid_spec=pltpu.PrefetchScalarGridSpec(
            num_scalar_prefetch=1,
            grid=(width // WIDE,),
            in_specs=[pl.BlockSpec((4, 2, 4, 8, depth), lambda i, core: (0, 0, 0, 0, 0))] * len(chunks)
            + [pl.BlockSpec((WIDE, depth), lambda i, core: (i, 0))] * 2,
            out_specs=pl.BlockSpec((rows, WIDE), lambda i, core: (0, i)),
            scratch_shapes=[pltpu.VMEM((2, 2 * rows, depth), jnp.bfloat16)],
        ),
        compiler_params=PARAMS,
        cost_estimate=COST,
    )(core, *chunks, *slabs)


def finish_body(y_ref, own_ref, sides_ref, across_ref, out_ref):
    me = y_ref[0]

    def put(offset, rows):
        out_ref[0, lax.rem(me + offset, 4)] = rows

    def summed(k):
        return (sides_ref[0, 0, k] + sides_ref[1, 0, k]) + (sides_ref[2, 0, k] + sides_ref[3, 0, k])

    put(0, own_ref[0])
    put(3, summed(0))
    put(1, summed(1))
    put(2, across_ref[0])


def finish(y, own, sides, across):
    total = pl.BlockSpec((1, 8, 1024), lambda low, y: (low, 0, 0))
    parts = pl.BlockSpec((4, 1, 2, 8, 1024), lambda low, y: (0, low, 0, 0, 0))
    return pl.pallas_call(
        finish_body,
        out_shape=jax.ShapeDtypeStruct((4, 4, 8, 1024), jnp.float32),
        grid_spec=pltpu.PrefetchScalarGridSpec(
            num_scalar_prefetch=1,
            grid=(4,),
            in_specs=[total, parts, total],
            out_specs=pl.BlockSpec((1, 4, 8, 1024), lambda low, y: (low, 0, 0, 0)),
        ),
        compiler_params=PARAMS,
        cost_estimate=COST,
    )(y, own, sides, across)


def around(value, hops):
    return lax.ppermute(value, "y", [(i, (i + hops) % 4) for i in range(4)])


def summed_over_x(partial):
    return lax.psum_scatter(partial, "x", scatter_dimension=0, tiled=True).reshape(4, 8, 1024)


def over_x(partial):
    return lax.all_to_all(partial.reshape(4, 4, -1, 8, 1024), "x", 0, 0)


def per_device(integrals, amplitudes, allowed):
    core = lax.axis_index("core").astype(jnp.int32)[None]
    me = lax.axis_index("y").astype(jnp.int32)[None]
    with jax.named_scope("slab"):
        kept = masked(integrals, allowed)
        slabs = (kept, lax.ppermute(kept, "core", [(0, 1), (1, 0)]))
    with jax.named_scope("gather_far"):
        far = lax.all_gather(amplitudes, "zh")
    with jax.named_scope("gather_near"):
        by_core = far.reshape(1, 4, 2, 8, 512).swapaxes(1, 2)
        spread = jnp.broadcast_to(by_core, (4, 2, 4, 8, 512)).reshape(8, 4, 8, 512)
        near = lax.all_to_all(spread, ("zl", "core"), 0, 0).reshape(4, 2, 4, 8, 512)
    with jax.named_scope("gather_y"):
        below, above = around(near, 1), around(near, 3)
        across = around(near, 2)
    with jax.named_scope("own_y"):
        own = summed_over_x(ladder(core, [near], slabs))
    with jax.named_scope("sides_y"):
        sides = over_x(ladder(core, [below, above], slabs))
    with jax.named_scope("across_y"):
        opposite = summed_over_x(ladder(core, [across], slabs))
    return finish(me, own, sides, opposite).reshape(128, 1024)


def solution(mesh):
    fine = Mesh(mesh.devices.reshape(8, 4, 4, 4, 2), ("zh", "zl", "y", "x", "core"))
    rows, cols = ("zh", "zl", "y"), ("x", "core")
    return jax.shard_map(
        per_device, mesh=fine, in_specs=(P(rows, cols),) * 3, out_specs=P(cols, rows), check_vma=False
    )
```

```python
import functools

import jax
import jax.numpy as jnp
from jax import lax
from jax.experimental import pallas as pl
from jax.experimental.pallas import tpu as pltpu
from jax.sharding import Mesh, PartitionSpec as P

BLK = 128
NT = (((1,), (1,)), ((), ()))
COLS = 256
WIDE = 512
PARAMS = pltpu.CompilerParams(vmem_limit_bytes=48 * 2**20)
COST = pl.CostEstimate(flops=1, bytes_accessed=1, transcendentals=0)


def split(wide):
    high = wide.astype(jnp.bfloat16)
    return high, (wide - high.astype(jnp.float32)).astype(jnp.bfloat16)


def mask_body(allowed_ref, v_ref, kept_ref):
    step = pl.program_id(0)
    for a in range(COLS // BLK):
        rows = pl.ds(a * BLK, BLK)
        for c in range(v_ref.shape[1] // BLK):
            cols = pl.ds(c * BLK, BLK)
            weight = allowed_ref[step * (COLS // BLK) + a, c].astype(jnp.float32)
            kept_ref[rows, cols] = v_ref[rows, cols] * weight


def masked(integrals, allowed):
    rows, depth = integrals.shape
    block = pl.BlockSpec((COLS, depth), lambda i, allowed: (i, 0))
    return pl.pallas_call(
        mask_body,
        out_shape=jax.ShapeDtypeStruct((rows, depth), jnp.float32),
        grid_spec=pltpu.PrefetchScalarGridSpec(
            num_scalar_prefetch=1, grid=(rows // COLS,), in_specs=[block], out_specs=block
        ),
        compiler_params=PARAMS,
        cost_estimate=COST,
    )(allowed, integrals)


def ladder_body(count, core_ref, *refs):
    t_refs, (own_ref, got_ref, out_ref, t_parts) = refs[:count], refs[count:]
    core = core_ref[0]
    size = 32 * count
    rows = 4 * size

    @pl.when(pl.program_id(0) == 0)
    def _():
        for side in range(2):
            source = core if side == 0 else 1 - core
            for xx in range(4):
                wide = jnp.concatenate([t[low, source, xx] for low in range(4) for t in t_refs], axis=0)
                high, low_part = split(wide)
                t_parts[side, pl.ds(xx * size, size), :] = high
                t_parts[side, pl.ds(rows + xx * size, size), :] = low_part

    def dot(left, right):
        return lax.dot_general(left, right, NT, preferred_element_type=jnp.float32)

    total = None
    for side, v_ref in enumerate((own_ref, got_ref)):
        high, low_part = split(v_ref[...])
        both = dot(t_parts[side], high)
        term = (both[rows:] + dot(t_parts[side, :rows], low_part)) + both[:rows]
        total = term if total is None else total + term
    out_ref[...] = total


def ladder(core, chunks, slabs):
    width, depth = slabs[0].shape
    rows = 128 * len(chunks)
    return pl.pallas_call(
        functools.partial(ladder_body, len(chunks)),
        out_shape=jax.ShapeDtypeStruct((rows, width), jnp.float32),
        grid_spec=pltpu.PrefetchScalarGridSpec(
            num_scalar_prefetch=1,
            grid=(width // WIDE,),
            in_specs=[pl.BlockSpec((4, 2, 4, 8, depth), lambda i, core: (0, 0, 0, 0, 0))] * len(chunks)
            + [pl.BlockSpec((WIDE, depth), lambda i, core: (i, 0))] * 2,
            out_specs=pl.BlockSpec((rows, WIDE), lambda i, core: (0, i)),
            scratch_shapes=[pltpu.VMEM((2, 2 * rows, depth), jnp.bfloat16)],
        ),
        compiler_params=PARAMS,
        cost_estimate=COST,
    )(core, *chunks, *slabs)


def finish_body(y_ref, own_ref, sides_ref, across_ref, out_ref):
    me = y_ref[0]

    def put(offset, part_ref, k):
        place = lax.rem(me + offset, 4)
        out_ref[0, place] = (part_ref[0, 0, k] + part_ref[1, 0, k]) + (part_ref[2, 0, k] + part_ref[3, 0, k])

    put(0, own_ref, 0)
    put(3, sides_ref, 0)
    put(1, sides_ref, 1)
    put(2, across_ref, 0)


def finish(y, own, sides, across):
    def part(count):
        return pl.BlockSpec((4, 1, count, 8, 1024), lambda low, y: (0, low, 0, 0, 0))

    return pl.pallas_call(
        finish_body,
        out_shape=jax.ShapeDtypeStruct((4, 4, 8, 1024), jnp.float32),
        grid_spec=pltpu.PrefetchScalarGridSpec(
            num_scalar_prefetch=1,
            grid=(4,),
            in_specs=[part(1), part(2), part(1)],
            out_specs=pl.BlockSpec((1, 4, 8, 1024), lambda low, y: (low, 0, 0, 0)),
        ),
        compiler_params=PARAMS,
        cost_estimate=COST,
    )(y, own, sides, across)


def around(value, hops):
    return lax.ppermute(value, "y", [(i, (i + hops) % 4) for i in range(4)])


def over_x(partial):
    return lax.all_to_all(partial.reshape(4, 4, -1, 8, 1024), "x", 0, 0)


def per_device(integrals, amplitudes, allowed):
    core = lax.axis_index("core").astype(jnp.int32)[None]
    me = lax.axis_index("y").astype(jnp.int32)[None]
    with jax.named_scope("slab"):
        kept = masked(integrals, allowed)
        slabs = (kept, lax.ppermute(kept, "core", [(0, 1), (1, 0)]))
    with jax.named_scope("gather_far"):
        far = lax.all_gather(amplitudes, "zh")
    with jax.named_scope("gather_near"):
        by_core = far.reshape(1, 4, 2, 8, 512).swapaxes(1, 2)
        spread = jnp.broadcast_to(by_core, (4, 2, 4, 8, 512)).reshape(8, 4, 8, 512)
        near = lax.all_to_all(spread, ("zl", "core"), 0, 0).reshape(4, 2, 4, 8, 512)
    with jax.named_scope("gather_y"):
        below, above = around(near, 1), around(near, 3)
        across = around(near, 2)
    with jax.named_scope("own_y"):
        own = over_x(ladder(core, [near], slabs))
    with jax.named_scope("sides_y"):
        sides = over_x(ladder(core, [below, above], slabs))
    with jax.named_scope("across_y"):
        opposite = over_x(ladder(core, [across], slabs))
    return finish(me, own, sides, opposite).reshape(128, 1024)


def solution(mesh):
    fine = Mesh(mesh.devices.reshape(8, 4, 4, 4, 2), ("zh", "zl", "y", "x", "core"))
    rows, cols = ("zh", "zl", "y"), ("x", "core")
    return jax.shard_map(
        per_device, mesh=fine, in_specs=(P(rows, cols),) * 3, out_specs=P(cols, rows), check_vma=False
    )
```

```python
import functools

import jax
import jax.numpy as jnp
from jax import lax
from jax.experimental import pallas as pl
from jax.experimental.pallas import tpu as pltpu
from jax.sharding import Mesh, PartitionSpec as P

BLK = 128
NT = (((1,), (1,)), ((), ()))
COLS = 256
WIDE = 512
PARAMS = pltpu.CompilerParams(vmem_limit_bytes=48 * 2**20)
COST = pl.CostEstimate(flops=1, bytes_accessed=1, transcendentals=0)


def split(wide):
    high = wide.astype(jnp.bfloat16)
    return high, (wide - high.astype(jnp.float32)).astype(jnp.bfloat16)


def mask_body(allowed_ref, v_ref, kept_ref):
    step = pl.program_id(0)
    for a in range(COLS // BLK):
        rows = pl.ds(a * BLK, BLK)
        for c in range(v_ref.shape[1] // BLK):
            cols = pl.ds(c * BLK, BLK)
            weight = allowed_ref[step * (COLS // BLK) + a, c].astype(jnp.float32)
            kept_ref[rows, cols] = v_ref[rows, cols] * weight


def masked(integrals, allowed):
    rows, depth = integrals.shape
    block = pl.BlockSpec((COLS, depth), lambda i, allowed: (i, 0))
    return pl.pallas_call(
        mask_body,
        out_shape=jax.ShapeDtypeStruct((rows, depth), jnp.float32),
        grid_spec=pltpu.PrefetchScalarGridSpec(
            num_scalar_prefetch=1, grid=(rows // COLS,), in_specs=[block], out_specs=block
        ),
        compiler_params=PARAMS,
        cost_estimate=COST,
    )(allowed, integrals)


def ladder_body(count, core_ref, *refs):
    t_refs, (own_ref, got_ref, out_ref, t_parts) = refs[:count], refs[count:]
    core = core_ref[0]
    size = 32 * count
    rows = 4 * size

    @pl.when(pl.program_id(0) == 0)
    def _():
        for side in range(2):
            source = core if side == 0 else 1 - core
            for xx in range(4):
                wide = jnp.concatenate([t[low, source, xx] for low in range(4) for t in t_refs], axis=0)
                high, low_part = split(wide)
                t_parts[side, pl.ds(xx * size, size), :] = high
                t_parts[side, pl.ds(rows + xx * size, size), :] = low_part

    def dot(left, right):
        return lax.dot_general(left, right, NT, preferred_element_type=jnp.float32)

    total = None
    for side, v_ref in enumerate((own_ref, got_ref)):
        high, low_part = split(v_ref[...])
        both = dot(t_parts[side], high)
        term = (both[rows:] + dot(t_parts[side, :rows], low_part)) + both[:rows]
        total = term if total is None else total + term
    out_ref[...] = total


def ladder(core, chunks, slabs):
    width, depth = slabs[0].shape
    rows = 128 * len(chunks)
    return pl.pallas_call(
        functools.partial(ladder_body, len(chunks)),
        out_shape=jax.ShapeDtypeStruct((rows, width), jnp.float32),
        grid_spec=pltpu.PrefetchScalarGridSpec(
            num_scalar_prefetch=1,
            grid=(width // WIDE,),
            in_specs=[pl.BlockSpec((4, 2, 4, 8, depth), lambda i, core: (0, 0, 0, 0, 0))] * len(chunks)
            + [pl.BlockSpec((WIDE, depth), lambda i, core: (i, 0))] * 2,
            out_specs=pl.BlockSpec((rows, WIDE), lambda i, core: (0, i)),
            scratch_shapes=[pltpu.VMEM((2, 2 * rows, depth), jnp.bfloat16)],
        ),
        compiler_params=PARAMS,
        cost_estimate=COST,
    )(core, *chunks, *slabs)


def finish_body(y_ref, own_ref, sides_ref, across_ref, out_ref):
    me = y_ref[0]

    def put(bits, part_ref, k):
        place = lax.bitwise_xor(me, bits)
        out_ref[0, place] = (part_ref[0, 0, k] + part_ref[1, 0, k]) + (part_ref[2, 0, k] + part_ref[3, 0, k])

    put(0, own_ref, 0)
    put(1, sides_ref, 0)
    put(3, sides_ref, 1)
    put(2, across_ref, 0)


def finish(y, own, sides, across):
    def part(count):
        return pl.BlockSpec((4, 1, count, 8, 1024), lambda low, y: (0, low, 0, 0, 0))

    return pl.pallas_call(
        finish_body,
        out_shape=jax.ShapeDtypeStruct((4, 4, 8, 1024), jnp.float32),
        grid_spec=pltpu.PrefetchScalarGridSpec(
            num_scalar_prefetch=1,
            grid=(4,),
            in_specs=[part(1), part(2), part(1)],
            out_specs=pl.BlockSpec((1, 4, 8, 1024), lambda low, y: (low, 0, 0, 0)),
        ),
        compiler_params=PARAMS,
        cost_estimate=COST,
    )(y, own, sides, across)


def swapped(value, bits):
    return lax.ppermute(value, "y", [(i, i ^ bits) for i in range(4)])


def over_x(partial):
    return lax.all_to_all(partial.reshape(4, 4, -1, 8, 1024), "x", 0, 0)


def per_device(integrals, amplitudes, allowed):
    core = lax.axis_index("core").astype(jnp.int32)[None]
    me = lax.axis_index("y").astype(jnp.int32)[None]
    with jax.named_scope("slab"):
        kept = masked(integrals, allowed)
        slabs = (kept, lax.ppermute(kept, "core", [(0, 1), (1, 0)]))
    with jax.named_scope("gather_far"):
        far = lax.all_gather(amplitudes, "zh")
    with jax.named_scope("gather_near"):
        by_core = far.reshape(1, 4, 2, 8, 512).swapaxes(1, 2)
        spread = jnp.broadcast_to(by_core, (4, 2, 4, 8, 512)).reshape(8, 4, 8, 512)
        near = lax.all_to_all(spread, ("zl", "core"), 0, 0).reshape(4, 2, 4, 8, 512)
    with jax.named_scope("gather_y"):
        first, second = swapped(near, 1), swapped(near, 3)
        across = swapped(near, 2)
    with jax.named_scope("own_y"):
        own = over_x(ladder(core, [near], slabs))
    with jax.named_scope("sides_y"):
        sides = over_x(ladder(core, [first, second], slabs))
    with jax.named_scope("across_y"):
        opposite = over_x(ladder(core, [across], slabs))
    return finish(me, own, sides, opposite).reshape(128, 1024)


def solution(mesh):
    fine = Mesh(mesh.devices.reshape(8, 4, 4, 4, 2), ("zh", "zl", "y", "x", "core"))
    rows, cols = ("zh", "zl", "y"), ("x", "core")
    return jax.shard_map(
        per_device, mesh=fine, in_specs=(P(rows, cols),) * 3, out_specs=P(cols, rows), check_vma=False
    )
```

```python
import functools

import jax
import jax.numpy as jnp
from jax import lax
from jax.experimental import pallas as pl
from jax.experimental.pallas import tpu as pltpu
from jax.sharding import Mesh, PartitionSpec as P

BLK = 128
NT = (((1,), (1,)), ((), ()))
COLS = 256
WIDE = 512
PARAMS = pltpu.CompilerParams(vmem_limit_bytes=48 * 2**20)
COST = pl.CostEstimate(flops=1, bytes_accessed=1, transcendentals=0)


def split(wide):
    high = wide.astype(jnp.bfloat16)
    return high, (wide - high.astype(jnp.float32)).astype(jnp.bfloat16)


def mask_body(allowed_ref, v_ref, kept_ref):
    step = pl.program_id(0)
    for a in range(COLS // BLK):
        rows = pl.ds(a * BLK, BLK)
        for c in range(v_ref.shape[1] // BLK):
            cols = pl.ds(c * BLK, BLK)
            weight = allowed_ref[step * (COLS // BLK) + a, c].astype(jnp.float32)
            kept_ref[rows, cols] = v_ref[rows, cols] * weight


def masked(integrals, allowed):
    rows, depth = integrals.shape
    block = pl.BlockSpec((COLS, depth), lambda i, allowed: (i, 0))
    return pl.pallas_call(
        mask_body,
        out_shape=jax.ShapeDtypeStruct((rows, depth), jnp.float32),
        grid_spec=pltpu.PrefetchScalarGridSpec(
            num_scalar_prefetch=1, grid=(rows // COLS,), in_specs=[block], out_specs=block
        ),
        compiler_params=PARAMS,
        cost_estimate=COST,
    )(allowed, integrals)


def ladder_body(count, core_ref, *refs):
    t_refs, (own_ref, got_ref, out_ref, t_parts) = refs[:count], refs[count:]
    core = core_ref[0]
    size = 32 * count
    rows = 4 * size

    @pl.when(pl.program_id(0) == 0)
    def _():
        for side in range(2):
            source = core if side == 0 else 1 - core
            for xx in range(4):
                wide = jnp.concatenate([t[low, source, xx] for low in range(4) for t in t_refs], axis=0)
                high, low_part = split(wide)
                t_parts[side, pl.ds(xx * size, size), :] = high
                t_parts[side, pl.ds(rows + xx * size, size), :] = low_part

    def dot(left, right):
        return lax.dot_general(left, right, NT, preferred_element_type=jnp.float32)

    total = None
    for side, v_ref in enumerate((own_ref, got_ref)):
        high, low_part = split(v_ref[...])
        both = dot(t_parts[side], high)
        term = (both[rows:] + dot(t_parts[side, :rows], low_part)) + both[:rows]
        total = term if total is None else total + term
    out_ref[...] = total


def ladder(core, chunks, slabs):
    width, depth = slabs[0].shape
    rows = 128 * len(chunks)
    return pl.pallas_call(
        functools.partial(ladder_body, len(chunks)),
        out_shape=jax.ShapeDtypeStruct((rows, width), jnp.float32),
        grid_spec=pltpu.PrefetchScalarGridSpec(
            num_scalar_prefetch=1,
            grid=(width // WIDE,),
            in_specs=[pl.BlockSpec((4, 2, 4, 8, depth), lambda i, core: (0, 0, 0, 0, 0))] * len(chunks)
            + [pl.BlockSpec((WIDE, depth), lambda i, core: (i, 0))] * 2,
            out_specs=pl.BlockSpec((rows, WIDE), lambda i, core: (0, i)),
            scratch_shapes=[pltpu.VMEM((2, 2 * rows, depth), jnp.bfloat16)],
        ),
        compiler_params=pltpu.CompilerParams(vmem_limit_bytes=32 * 2**20),
        cost_estimate=COST,
    )(core, *chunks, *slabs)


def finish_body(y_ref, own_ref, sides_ref, across_ref, out_ref):
    me = y_ref[0]

    def put(bits, part_ref, k):
        place = lax.bitwise_xor(me, bits)
        for low in range(2):
            a, b, c, d = (part_ref[x, low, k] for x in range(4))
            out_ref[low, place] = (a + b) + (c + d)

    put(0, own_ref, 0)
    put(1, sides_ref, 0)
    put(3, sides_ref, 1)
    put(2, across_ref, 0)


def finish(y, own, sides, across):
    def part(count):
        return pl.BlockSpec((4, 2, count, 8, 1024), lambda low, y: (0, low, 0, 0, 0))

    return pl.pallas_call(
        finish_body,
        out_shape=jax.ShapeDtypeStruct((4, 4, 8, 1024), jnp.float32),
        grid_spec=pltpu.PrefetchScalarGridSpec(
            num_scalar_prefetch=1,
            grid=(2,),
            in_specs=[part(1), part(2), part(1)],
            out_specs=pl.BlockSpec((2, 4, 8, 1024), lambda low, y: (low, 0, 0, 0)),
        ),
        compiler_params=PARAMS,
        cost_estimate=COST,
    )(y, own, sides, across)


def swapped(value, bits):
    return lax.ppermute(value, "y", [(i, i ^ bits) for i in range(4)])


def over_x(partial):
    return lax.all_to_all(partial.reshape(4, 4, -1, 8, 1024), "x", 0, 0)


def per_device(integrals, amplitudes, allowed):
    core = lax.axis_index("core").astype(jnp.int32)[None]
    me = lax.axis_index("y").astype(jnp.int32)[None]
    with jax.named_scope("slab"):
        kept = masked(integrals, allowed)
        slabs = (kept, lax.ppermute(kept, "core", [(0, 1), (1, 0)]))
    with jax.named_scope("gather_far"):
        far = lax.all_gather(amplitudes, "zh")
    with jax.named_scope("gather_near"):
        by_core = far.reshape(1, 4, 2, 8, 512).swapaxes(1, 2)
        spread = jnp.broadcast_to(by_core, (4, 2, 4, 8, 512)).reshape(8, 4, 8, 512)
        near = lax.all_to_all(spread, ("zl", "core"), 0, 0).reshape(4, 2, 4, 8, 512)
    with jax.named_scope("gather_y"):
        first, second = swapped(near, 1), swapped(near, 3)
        across = swapped(near, 2)
    with jax.named_scope("own_y"):
        own = over_x(ladder(core, [near], slabs))
    with jax.named_scope("sides_y"):
        sides = over_x(ladder(core, [first, second], slabs))
    with jax.named_scope("across_y"):
        opposite = over_x(ladder(core, [across], slabs))
    return finish(me, own, sides, opposite).reshape(128, 1024)


def solution(mesh):
    fine = Mesh(mesh.devices.reshape(8, 4, 4, 4, 2), ("zh", "zl", "y", "x", "core"))
    rows, cols = ("zh", "zl", "y"), ("x", "core")
    return jax.shard_map(
        per_device, mesh=fine, in_specs=(P(rows, cols),) * 3, out_specs=P(cols, rows), check_vma=False
    )
```

```python
import functools

import jax
import jax.numpy as jnp
from jax import lax
from jax.experimental import pallas as pl
from jax.experimental.pallas import tpu as pltpu
from jax.sharding import Mesh, PartitionSpec as P

BLK = 128
NT = (((1,), (1,)), ((), ()))
COLS = 256
WIDE = 1024
PARAMS = pltpu.CompilerParams(vmem_limit_bytes=48 * 2**20)
COST = pl.CostEstimate(flops=1, bytes_accessed=1, transcendentals=0)


def split(wide):
    high = wide.astype(jnp.bfloat16)
    return high, (wide - high.astype(jnp.float32)).astype(jnp.bfloat16)


def mask_body(allowed_ref, v_ref, kept_ref):
    step = pl.program_id(0)
    for a in range(COLS // BLK):
        rows = pl.ds(a * BLK, BLK)
        for c in range(v_ref.shape[1] // BLK):
            cols = pl.ds(c * BLK, BLK)
            weight = allowed_ref[step * (COLS // BLK) + a, c].astype(jnp.float32)
            kept_ref[rows, cols] = v_ref[rows, cols] * weight


def masked(integrals, allowed):
    rows, depth = integrals.shape
    block = pl.BlockSpec((COLS, depth), lambda i, allowed: (i, 0))
    return pl.pallas_call(
        mask_body,
        out_shape=jax.ShapeDtypeStruct((rows, depth), jnp.float32),
        grid_spec=pltpu.PrefetchScalarGridSpec(
            num_scalar_prefetch=1, grid=(rows // COLS,), in_specs=[block], out_specs=block
        ),
        compiler_params=PARAMS,
        cost_estimate=COST,
    )(allowed, integrals)


def ladder_body(count, core_ref, *refs):
    t_refs, (own_ref, got_ref, out_ref, t_parts) = refs[:count], refs[count:]
    core = core_ref[0]
    size = 32 * count
    rows = 4 * size

    @pl.when(pl.program_id(0) == 0)
    def _():
        for side in range(2):
            source = core if side == 0 else 1 - core
            for xx in range(4):
                wide = jnp.concatenate([t[low, source, xx] for low in range(4) for t in t_refs], axis=0)
                high, low_part = split(wide)
                t_parts[side, pl.ds(xx * size, size), :] = high
                t_parts[side, pl.ds(rows + xx * size, size), :] = low_part

    def dot(left, right):
        return lax.dot_general(left, right, NT, preferred_element_type=jnp.float32)

    total = None
    for side, v_ref in enumerate((own_ref, got_ref)):
        high, low_part = split(v_ref[...])
        both = dot(t_parts[side], high)
        term = (both[rows:] + dot(t_parts[side, :rows], low_part)) + both[:rows]
        total = term if total is None else total + term
    out_ref[...] = total


def ladder(core, chunks, slabs):
    width, depth = slabs[0].shape
    rows = 128 * len(chunks)
    return pl.pallas_call(
        functools.partial(ladder_body, len(chunks)),
        out_shape=jax.ShapeDtypeStruct((rows, width), jnp.float32),
        grid_spec=pltpu.PrefetchScalarGridSpec(
            num_scalar_prefetch=1,
            grid=(width // WIDE,),
            in_specs=[pl.BlockSpec((4, 2, 4, 8, depth), lambda i, core: (0, 0, 0, 0, 0))] * len(chunks)
            + [pl.BlockSpec((WIDE, depth), lambda i, core: (i, 0))] * 2,
            out_specs=pl.BlockSpec((rows, WIDE), lambda i, core: (0, i)),
            scratch_shapes=[pltpu.VMEM((2, 2 * rows, depth), jnp.bfloat16)],
        ),
        compiler_params=pltpu.CompilerParams(vmem_limit_bytes=48 * 2**20),
        cost_estimate=COST,
    )(core, *chunks, *slabs)


def finish_body(y_ref, own_ref, sides_ref, across_ref, out_ref):
    me = y_ref[0]

    def put(bits, part_ref, k):
        place = lax.bitwise_xor(me, bits)
        for low in range(2):
            a, b, c, d = (part_ref[x, low, k] for x in range(4))
            out_ref[low, place] = (a + b) + (c + d)

    put(0, own_ref, 0)
    put(1, sides_ref, 0)
    put(3, sides_ref, 1)
    put(2, across_ref, 0)


def finish(y, own, sides, across):
    def part(count):
        return pl.BlockSpec((4, 2, count, 8, 1024), lambda low, y: (0, low, 0, 0, 0))

    return pl.pallas_call(
        finish_body,
        out_shape=jax.ShapeDtypeStruct((4, 4, 8, 1024), jnp.float32),
        grid_spec=pltpu.PrefetchScalarGridSpec(
            num_scalar_prefetch=1,
            grid=(2,),
            in_specs=[part(1), part(2), part(1)],
            out_specs=pl.BlockSpec((2, 4, 8, 1024), lambda low, y: (low, 0, 0, 0)),
        ),
        compiler_params=PARAMS,
        cost_estimate=COST,
    )(y, own, sides, across)


def swapped(value, bits):
    return lax.ppermute(value, "y", [(i, i ^ bits) for i in range(4)])


def over_x(partial):
    return lax.all_to_all(partial.reshape(4, 4, -1, 8, 1024), "x", 0, 0)


def per_device(integrals, amplitudes, allowed):
    core = lax.axis_index("core").astype(jnp.int32)[None]
    me = lax.axis_index("y").astype(jnp.int32)[None]
    with jax.named_scope("slab"):
        kept = masked(integrals, allowed)
        slabs = (kept, lax.ppermute(kept, "core", [(0, 1), (1, 0)]))
    with jax.named_scope("gather_far"):
        far = lax.all_gather(amplitudes, "zh")
    with jax.named_scope("gather_near"):
        by_core = far.reshape(1, 4, 2, 8, 512).swapaxes(1, 2)
        spread = jnp.broadcast_to(by_core, (4, 2, 4, 8, 512)).reshape(8, 4, 8, 512)
        near = lax.all_to_all(spread, ("zl", "core"), 0, 0).reshape(4, 2, 4, 8, 512)
    with jax.named_scope("gather_y"):
        first, second = swapped(near, 1), swapped(near, 3)
        across = swapped(near, 2)
    with jax.named_scope("own_y"):
        own = over_x(ladder(core, [near], slabs))
    with jax.named_scope("sides_y"):
        sides = over_x(ladder(core, [first, second], slabs))
    with jax.named_scope("across_y"):
        opposite = over_x(ladder(core, [across], slabs))
    return finish(me, own, sides, opposite).reshape(128, 1024)


def solution(mesh):
    fine = Mesh(mesh.devices.reshape(8, 4, 4, 4, 2), ("zh", "zl", "y", "x", "core"))
    rows, cols = ("zh", "zl", "y"), ("x", "core")
    return jax.shard_map(
        per_device, mesh=fine, in_specs=(P(rows, cols),) * 3, out_specs=P(cols, rows), check_vma=False
    )
```
